128 devices in a mesh: expert: 32 (over x, z, core), tensor: 4 (over y).
Axes of the slice: x: 4, y: 4, z: 4, core: 2. Of those that a mesh axis runs over, the one named last changes fastest.
Arguments:
- query_nope: bfloat16 [1024, 16384], P('expert', 'tensor'), may hold values from -6 to 6
- query_rope: bfloat16 [1024, 8192], P('expert', 'tensor'), may hold values from -14 to 14
- key_absorb: bfloat16 [128, 128, 512], P('tensor'), may hold values from -0.5 to 0.5
- latent_cache: bfloat16 [1024, 512, 576], P(('expert', 'tensor')), may hold values from -4 to 4
- new_latent: bfloat16 [1024, 576], P(('expert', 'tensor')), may hold values from -6 to 6
- context_lengths: int32 [1024], P(('expert', 'tensor')), may hold values from 2 to 512
- value_absorb: bfloat16 [128, 512, 128], P('tensor'), may hold values from -0.25 to 0.25
- out_proj: bfloat16 [16384, 7168], P('tensor', 'expert'), may hold values from -0.1875 to 0.1875
- residual: bfloat16 [1024, 7168], P(('expert', 'tensor')), may hold values from -6 to 6
- norm_gain: bfloat16 [7168], replicated, may hold values from 0.099609375 to 1.8984375
- routes: int32 [1024, 8], P(('expert', 'tensor')), may hold values from 0 to 31, all different within a row; in each aligned block of 8 rows (0 to 7, 8 to 15, ...) at most 4 rows name the same one
- gate_weights: float32 [1024, 8], P(('expert', 'tensor')), may hold values from 0.1 to 1
- expert_gate: bfloat16 [32, 7168, 1024], P('expert', None, 'tensor'), may hold values from -0.0625 to 0.0625
- expert_up: bfloat16 [32, 7168, 1024], P('expert', None, 'tensor'), may hold values from -0.0625 to 0.0625
- expert_down: bfloat16 [32, 1024, 7168], P('expert', 'tensor'), may hold values from -0.1875 to 0.1875
Outputs:
- layer_out: bfloat16 [1024, 7168], P(('expert', 'tensor'))
The draws below stay inside these ranges and needn't reach their ends.
Inputs may be any that keep to these rules, and one draw needn't show every extreme that they name: `routes`: in each aligned block of 8 rows (the rows of one device) no expert is named by more than 4 rows, a bound that some block reaches.
All inputs are finite; a program needn't handle non-finite values.
Results may differ from the reference program's by a relative error of at most 0.02.
Values may be sent and summed in bfloat16 or wider, within the bound.
A program may use at most 128 MiB of HBM per device.

```python
import math
import jax
import jax.numpy as jnp
import numpy as np
from jax import lax

D = 7168
HEADS = 128
NOPE = 128
ROPE = 64
LATENT = 512
VHEAD = 128
TOPK = 8
FF = 1024
REQ_DEV = 8
CTX = 512
TOKENS = 1024
EXPERTS = 32
CAP = 4
N_EXPERT = 32
N_TENSOR = 4


def draw_latent_cache(key, part):
    key = jax.random.fold_in(key, 11)
    full_width = LATENT + ROPE
    values = jax.random.truncated_normal(key, -4.0, 4.0, (TOKENS, CTX, full_width), jnp.float32)
    return values.astype(jnp.bfloat16)


def draw_query_rope(key, part):
    key = jax.random.fold_in(key, 12)
    values = jax.random.truncated_normal(key, -4.0, 4.0, (TOKENS, HEADS, ROPE), jnp.float32)
    return values.reshape(TOKENS, HEADS * ROPE).astype(jnp.bfloat16)


def draw_context_lengths(key, part):
    key = jax.random.fold_in(key, 13)
    draw_one = jax.random.randint(jax.random.fold_in(key, 1), (TOKENS,), 2, CTX + 1, jnp.int32)
    draw_two = jax.random.randint(jax.random.fold_in(key, 2), (TOKENS,), 2, CTX + 1, jnp.int32)
    lengths = jnp.minimum(draw_one, draw_two)
    request = lax.broadcasted_iota(jnp.int32, (TOKENS,), 0)
    return jnp.where(request == 0, CTX, lengths).astype(jnp.int32)


def block_levels(stream_key, shape, split, smallest, largest):
    def one(dim, parts):
        heights = jax.random.uniform(jax.random.fold_in(jax.random.fold_in(stream_key, 6), dim), (parts,), jnp.float32, smallest / len(split), largest / len(split))
        return jnp.repeat(jnp.exp(heights), shape[dim] // parts).reshape((-1,) + (1,) * (len(shape) - dim - 1))

    loudness = one(*split[0])
    for cut in split[1:]:
        loudness = loudness * one(*cut)
    return loudness


def deal_out(own_key, own, number, rows, number_of, top, reach, lean):
    ranking = jax.random.permutation(own_key, number_of)
    packed, common = portions_of(number_of, rows * top, reach, lean, True), portions_of(number_of, rows * top, reach, lean, False)
    places = jnp.arange(number_of)

    def named(sizes, offset_by):
        used = int((sizes > 0).sum())
        fixed = max(1, used // 4)
        passed = fixed + (places - fixed + offset_by * (used - fixed)) % max(1, number_of - fixed)
        return jnp.zeros((number_of,), jnp.int32).at[ranking[jnp.where(places < fixed, places, passed)]].set(jnp.asarray(sizes, jnp.int32))

    sizes = jnp.where(number % 4 == 0, named(packed, number // 4), named(common, number - number // 4 - 1))
    mixed = jax.random.permutation(jax.random.fold_in(own, 3), number_of)
    donor, taker = mixed[0:number_of // 2 * 2:2], mixed[1:number_of // 2 * 2:2]
    room = jnp.minimum(sizes[donor] - 1, reach - sizes[taker]) // 2
    room = jnp.where((donor == ranking[0]) | (taker == ranking[0]) | (sizes[taker] == 0), 0, jnp.maximum(room, 0))
    passed = jax.random.randint(jax.random.fold_in(own, 4), (number_of // 2,), 0, 1 << 20) % (room + 1)
    sizes = sizes.at[donor].add(-passed).at[taker].add(passed)
    items = jnp.searchsorted(jnp.cumsum(sizes), jnp.arange(rows * top), side="right").astype(jnp.int32)
    listing = items.reshape(top, rows).T
    listing = listing[jax.random.permutation(jax.random.fold_in(own, 1), rows)]
    offset_by = jax.random.randint(jax.random.fold_in(own, 2), (rows, 1), 0, top)
    return jnp.take_along_axis(listing, (jnp.arange(top)[None, :] + offset_by) % top, axis=1)


def portions_of(count, total, reach, skew, full):
    weights = [(1 << 20) // math.isqrt(standing ** skew) + 1 for standing in range(1, count + 1)]
    largest = reach if full else min(reach, max(-(-total // count), total * weights[0] // sum(weights)))
    least = 1 if total - largest >= count - 1 else 0
    counts, spare = [largest] + [least] * (count - 1), total - largest - least * (count - 1)
    while spare > 0:
        movable = [i for i in range(1, count) if counts[i] < largest] or [i for i in range(1, count) if counts[i] < reach]
        pool, left = sum([weights[i] for i in movable]), spare
        for i in movable:
            extra = min(reach - counts[i], max(1, left * weights[i] // pool), spare)
            counts[i] = counts[i] + extra
            spare = spare - extra
    return np.array(counts)


def centred(key, dims, deviation, bound, cuts=(), kind=jnp.bfloat16):
    loudness = block_levels(key, dims, cuts, -0.22, 0.18) if cuts else 1.0
    array = jax.random.normal(key, dims, jnp.float32) * deviation * loudness
    return jnp.minimum(jnp.maximum(array, -bound), bound).astype(kind)


def setup_inputs(seed: int = 0) -> dict:
    seeds = jax.random.split(jax.random.key(seed), 16)
    query_nope = centred(seeds[0], (TOKENS, HEADS * NOPE), 1.0, 6.0, ((0, 32), (1, 4)))
    query_rope = draw_query_rope(jax.random.fold_in(seeds[15], 71), 0)
    key_absorb = centred(seeds[2], (HEADS, NOPE, LATENT), NOPE ** -0.5, 0.5, ((0, 4),))
    latent_cache = draw_latent_cache(jax.random.fold_in(seeds[15], 71), 0)
    new_latent = centred(seeds[4], (TOKENS, LATENT + ROPE), 1.0, 6.0, ((0, 128),))
    context_lengths = draw_context_lengths(jax.random.fold_in(seeds[15], 71), 0)
    value_absorb = centred(seeds[6], (HEADS, LATENT, VHEAD), LATENT ** -0.5, 0.25, ((0, 4),))
    out_proj = centred(seeds[7], (HEADS * VHEAD, D), (HEADS * VHEAD // 16) ** -0.5, 0.1875, ((0, 4), (1, 32)))
    residual = centred(seeds[8], (TOKENS, D), 1.0, 6.0, ((0, 128),))
    norm_gain = jnp.clip(1.0 + 0.18 * jax.random.normal(seeds[9], (D,), jnp.float32), 0.099609375, 1.8984375).astype(jnp.bfloat16)
    routes_keys = jax.random.split(jax.random.fold_in(seeds[10], 1), TOKENS // REQ_DEV)
    routes_turns = jax.random.permutation(jax.random.fold_in(seeds[10], 3), TOKENS // REQ_DEV)
    routes = jax.vmap(lambda own, number: deal_out(jax.random.fold_in(seeds[10], 2), own, number, REQ_DEV, EXPERTS, TOPK, CAP, 2))(routes_keys, routes_turns).reshape((TOKENS, TOPK))
    gate_weights = jnp.clip(jnp.exp(math.log(1.0) - 2.3025851 * jax.random.uniform(seeds[11], (TOKENS, TOPK), jnp.float32) ** block_levels(seeds[11], (TOKENS, TOPK), ((0, 128),), -0.2, 0.2)), 0.1, 1.0)
    expert_gate = centred(seeds[12], (EXPERTS, D, FF), D ** -0.5, 0.0625, ((0, 32), (2, 4)))
    expert_up = centred(seeds[13], (EXPERTS, D, FF), D ** -0.5, 0.0625, ((0, 32), (2, 4)))
    expert_down = centred(seeds[14], (EXPERTS, FF, D), FF ** -0.5, 0.1875, ((0, 32), (1, 4)))
    return {"query_nope": query_nope, "query_rope": query_rope, "key_absorb": key_absorb, "latent_cache": latent_cache, "new_latent": new_latent, "context_lengths": context_lengths, "value_absorb": value_absorb, "out_proj": out_proj, "residual": residual, "norm_gain": norm_gain, "routes": routes, "gate_weights": gate_weights, "expert_gate": expert_gate, "expert_up": expert_up, "expert_down": expert_down}


def reference(query_nope, query_rope, key_absorb, latent_cache, new_latent, context_lengths, value_absorb, out_proj, residual, norm_gain, routes, gate_weights, expert_gate, expert_up, expert_down):
    nope_rows = query_nope.reshape(TOKENS, HEADS, NOPE).astype(jnp.float32)
    absorbed = jnp.einsum('rhn,hnl->rhl', nope_rows, key_absorb.astype(jnp.float32)).astype(jnp.bfloat16)
    rope_rows = query_rope.reshape(TOKENS, HEADS, ROPE)
    queries = jnp.concatenate([absorbed, rope_rows], axis=2)
    score_scale = 1.0 / math.sqrt(NOPE + ROPE)

    def attend(pieces):
        query_rows, cache_rows, fresh_row, length = pieces
        scores = jnp.dot(query_rows, cache_rows.T, preferred_element_type=jnp.float32) * score_scale
        own_score = jnp.dot(query_rows, fresh_row, preferred_element_type=jnp.float32) * score_scale
        in_range = jnp.arange(CTX, dtype=jnp.int32) < length
        scores = jnp.where(in_range[None, :], scores, -jnp.inf)
        row_max = jnp.maximum(lax.optimization_barrier(jnp.max(scores, axis=1)), own_score)
        exp_scores = jnp.exp(scores - row_max[:, None])
        own_expo = jnp.exp(own_score - row_max)
        denom_sum = lax.optimization_barrier(jnp.sum(exp_scores, axis=1)) + own_expo
        weights = (exp_scores / denom_sum[:, None]).astype(jnp.bfloat16)
        own_weight = (own_expo / denom_sum).astype(jnp.bfloat16)
        attended = jnp.dot(weights, cache_rows[:, :LATENT], preferred_element_type=jnp.float32)
        attended = attended + own_weight.astype(jnp.float32)[:, None] * fresh_row[:LATENT].astype(jnp.float32)[None, :]
        return attended.astype(jnp.bfloat16)
    attended = lax.map(attend, (queries, latent_cache, new_latent, context_lengths))
    head_out = jnp.einsum('rhl,hlv->rhv', attended.astype(jnp.float32), value_absorb.astype(jnp.float32)).astype(jnp.bfloat16)
    head_out = head_out.reshape(TOKENS, HEADS * VHEAD)
    attn = jnp.dot(head_out, out_proj, preferred_element_type=jnp.float32).astype(jnp.bfloat16)
    hidden = residual.astype(jnp.float32) + attn.astype(jnp.float32)
    normed = hidden * lax.rsqrt(lax.optimization_barrier(jnp.mean(hidden * hidden, axis=1, keepdims=True)) + 1e-06)
    normed = (normed * norm_gain.astype(jnp.float32)[None, :]).astype(jnp.bfloat16)
    max_rows = min(TOKENS, N_EXPERT * N_TENSOR * CAP)
    block_width = FF // N_TENSOR

    def one_expert(running, pieces):
        expert_index, gate_matrix, up_matrix, down_matrix = pieces
        hit_pairs = routes == expert_index
        hit_rows = jnp.any(hit_pairs, axis=1)
        weight = lax.optimization_barrier(jnp.sum(jnp.where(hit_pairs, gate_weights, 0.0), axis=1))
        row_count = jnp.sum(hit_rows.astype(jnp.int32))
        picked = jnp.nonzero(hit_rows, size=max_rows, fill_value=0)[0].astype(jnp.int32)
        token_rows = normed[picked]
        gate_part = jnp.dot(token_rows, gate_matrix, preferred_element_type=jnp.float32)
        up_part = jnp.dot(token_rows, up_matrix, preferred_element_type=jnp.float32)
        activation = (jax.nn.silu(gate_part) * up_part).astype(jnp.bfloat16)
        block_sums = jnp.zeros((max_rows, D), jnp.float32)
        for block in range(N_TENSOR):
            share = jnp.dot(activation[:, block * block_width:(block + 1) * block_width], down_matrix[block * block_width:(block + 1) * block_width], preferred_element_type=jnp.float32)
            share = lax.optimization_barrier(share.astype(jnp.bfloat16))
            block_sums = block_sums + share.astype(jnp.float32)
        expert_rows = lax.optimization_barrier(block_sums.astype(jnp.bfloat16)).astype(jnp.float32)
        live_rows = jnp.arange(max_rows, dtype=jnp.int32) < row_count
        weighted = jnp.where(live_rows, weight[picked], 0.0)[:, None] * expert_rows
        return (running.at[picked].add(weighted), None)
    routed_sum, _ = lax.scan(one_expert, jnp.zeros((TOKENS, D), jnp.float32), (jnp.arange(EXPERTS, dtype=jnp.int32), expert_gate, expert_up, expert_down))
    return (hidden + routed_sum).astype(jnp.bfloat16)
```

```python
import math

import jax
import jax.numpy as jnp
from jax import lax
from jax.sharding import PartitionSpec as P


def per_device(
    query_nope,
    query_rope,
    key_absorb,
    latent_cache,
    new_latent,
    context_lengths,
    value_absorb,
    out_proj,
    residual,
    norm_gain,
    routes,
    gate_weights,
    expert_gate,
    expert_up,
    expert_down,
):
    expert_count = lax.axis_size("expert")
    tensor_count = lax.axis_size("tensor")
    local_heads = key_absorb.shape[0]
    nope_dim = key_absorb.shape[1]
    latent_dim = key_absorb.shape[2]
    rope_dim = query_rope.shape[1] // local_heads
    group_rows = query_nope.shape[0]
    requests = latent_cache.shape[0]
    context = latent_cache.shape[1]
    nope_query = query_nope.reshape(group_rows, local_heads, nope_dim)
    absorbed = jnp.einsum(
        "rhn,hnl->rhl", nope_query, key_absorb, preferred_element_type=jnp.float32
    ).astype(jnp.bfloat16)
    rope_query = query_rope.reshape(group_rows, local_heads, rope_dim)
    absorbed, rope_query = (
        lax.all_to_all(absorbed, "tensor", split_axis=0, concat_axis=1, tiled=True),
        lax.all_to_all(rope_query, "tensor", split_axis=0, concat_axis=1, tiled=True),
    )
    queries = jnp.concatenate([absorbed, rope_query], axis=2)
    score_scale = 1.0 / math.sqrt(nope_dim + rope_dim)
    scores = (
        jnp.einsum("rhc,rpc->rhp", queries, latent_cache, preferred_element_type=jnp.float32)
        * score_scale
    )
    own_score = (
        jnp.einsum("rhc,rc->rh", queries, new_latent, preferred_element_type=jnp.float32)
        * score_scale
    )
    in_range = lax.broadcasted_iota(jnp.int32, (requests, context), 1) < context_lengths[:, None]
    scores = jnp.where(in_range[:, None, :], scores, -jnp.inf)
    row_max = jnp.maximum(jnp.max(scores, axis=2), own_score)
    exp_scores = jnp.exp(scores - row_max[:, :, None])
    own_expo = jnp.exp(own_score - row_max)
    denom_sum = jnp.sum(exp_scores, axis=2) + own_expo
    weights = (exp_scores / denom_sum[:, :, None]).astype(jnp.bfloat16)
    own_weight = (own_expo / denom_sum).astype(jnp.bfloat16)
    attended = jnp.einsum(
        "rhp,rpl->rhl", weights, latent_cache[:, :, :latent_dim], preferred_element_type=jnp.float32
    )
    attended = attended + own_weight.astype(jnp.float32)[:, :, None] * new_latent[
        :, None, :latent_dim
    ].astype(jnp.float32)
    attended = attended.astype(jnp.bfloat16)
    attended = lax.all_to_all(attended, "tensor", split_axis=1, concat_axis=0, tiled=True)
    head_out = jnp.einsum(
        "rhl,hlv->rhv", attended, value_absorb, preferred_element_type=jnp.float32
    ).astype(jnp.bfloat16)
    head_out = head_out.reshape(group_rows, -1)
    partial_value = jnp.dot(
        lax.all_gather(head_out, "expert", axis=0, tiled=True),
        out_proj,
        preferred_element_type=jnp.float32,
    )
    local_width = out_proj.shape[1]
    partial_value = partial_value.astype(jnp.bfloat16).reshape(
        expert_count, tensor_count, requests, local_width
    )
    partial_value = jnp.swapaxes(partial_value, 0, 1).reshape(-1, local_width)
    summed = lax.psum_scatter(partial_value, "tensor", scatter_dimension=0, tiled=True)
    summed = summed.reshape(expert_count, requests, local_width)
    attn_rows = lax.all_to_all(
        summed, "expert", split_axis=0, concat_axis=2, tiled=True
    )[0]
    hidden = residual.astype(jnp.float32) + attn_rows.astype(jnp.float32)
    normed = hidden * lax.rsqrt(jnp.mean(hidden * hidden, axis=1, keepdims=True) + 1e-06)
    normed = (normed * norm_gain.astype(jnp.float32)[None, :]).astype(jnp.bfloat16)
    tokens = lax.all_gather(normed, ("expert", "tensor"), axis=0, tiled=True)
    experts = lax.broadcasted_iota(jnp.int32, (1, 1, expert_count), 2)
    table = jnp.sum(
        jnp.where(routes[:, :, None] == experts, gate_weights[:, :, None], 0.0), axis=1
    )
    table = lax.all_gather(table, ("expert", "tensor"), axis=0, tiled=True)
    mine = lax.broadcasted_iota(jnp.int32, (1, expert_count), 1) == lax.axis_index("expert")
    weight = jnp.sum(jnp.where(mine, table, 0.0), axis=1, keepdims=True)
    gate_part = jnp.dot(tokens, expert_gate[0], preferred_element_type=jnp.float32)
    up_part = jnp.dot(tokens, expert_up[0], preferred_element_type=jnp.float32)
    active = (jax.nn.silu(gate_part) * up_part * weight).astype(jnp.bfloat16)
    partial_out = jnp.dot(active, expert_down[0], preferred_element_type=jnp.float32)
    routed_sum = lax.psum_scatter(
        partial_out.astype(jnp.bfloat16), ("expert", "tensor"), scatter_dimension=0, tiled=True
    )
    return (hidden + routed_sum.astype(jnp.float32)).astype(jnp.bfloat16)


def solution(mesh):
    placed = (
        P("expert", "tensor"),
        P("expert", "tensor"),
        P("tensor", None, None),
        P(("expert", "tensor"), None, None),
        P(("expert", "tensor"), None),
        P(("expert", "tensor")),
        P("tensor", None, None),
        P("tensor", "expert"),
        P(("expert", "tensor"), None),
        P(),
        P(("expert", "tensor"), None),
        P(("expert", "tensor"), None),
        P("expert", None, "tensor"),
        P("expert", None, "tensor"),
        P("expert", "tensor", None),
    )
    return jax.shard_map(
        per_device,
        mesh=mesh,
        in_specs=placed,
        out_specs=P(("expert", "tensor"), None),
        check_vma=False,
    )
```

```python
import functools, math
import jax, jax.numpy as jnp
from jax import lax
from jax.experimental import pallas as pl
from jax.experimental.pallas import tpu as pltpu
from jax.sharding import PartitionSpec as P

MESH = pl.DeviceIdType.MESH
BF = jnp.bfloat16
F32 = jnp.float32
SIBLING = 6


def place():
    e, y = lax.axis_index("expert"), lax.axis_index("tensor")
    return e // 8, y, (e // 2) % 4, e % 2


def cube_bits(x, y, z):
    out = []
    for v in (y, x, z):
        g = jnp.where(v >= 2, 5 - v, v)
        out += [g // 2, g % 2]
    return out


def partner(x, y, z, c, d):
    if d == SIBLING:
        return ((x * 4 + z) * 2 + 1 - c, y)
    at = [y, x, z]
    v = at[d // 2]
    at[d // 2] = 3 - v if d % 2 == 0 else v + 1 - 2 * (v % 2)
    y, x, z = at
    return ((x * 4 + z) * 2 + c, y)


def meet(dims, x, y, z, c):
    barrier = pltpu.get_barrier_semaphore()
    for d in dims:
        pl.semaphore_signal(barrier, inc=1, device_id=partner(x, y, z, c, d), device_id_type=MESH)
    pl.semaphore_wait(barrier, len(dims))


OUT_W = (640, 640, 640, 640, 512, 512)
OUT_AT = (0, 640, 1280, 1920, 2560, 3072)


def moe_out_kernel(act, down, out, ps, rb, r0, r1, r2, r3, r4, r5, sib_s, sib_r, st_s, st_r, fin):
    x, y, z, c = place()
    bits = cube_bits(x, y, z)
    rs = (r0, r1, r2, r3, r4, r5)
    meet(range(7), x, y, z, c)
    sib = partner(x, y, z, c, SIBLING)

    def cut(ref, p, fixed, lead=()):
        idx = tuple(fixed[d] if d in fixed else slice(None) for d in range(6))
        return ref.at[lead + idx + (slice(None), pl.ds(OUT_AT[p], OUT_W[p]))]

    def product(p, which):
        b = 1 - bits[p] if which == 0 else bits[p]

        def one(side, carry):
            half = jnp.where(side == 0, 1 - c, c)
            rows = act[tuple(b if d == p else slice(None) for d in range(6))]
            rows = rows.reshape(512, 256)
            cols = pl.ds(pl.multiple_of(half * 3584 + OUT_AT[p], 128), OUT_W[p])
            got = jnp.dot(rows, down[:, cols], preferred_element_type=F32).astype(BF)
            cut(ps, p, {p: b}, (side,))[...] = got.reshape(2, 2, 2, 2, 2, 16, OUT_W[p])
            return carry

        lax.fori_loop(0, 2, one, 0)
        copy = pltpu.make_async_remote_copy(
            src_ref=cut(ps, p, {p: b}, (0,)), dst_ref=cut(rb, p, {p: b}),
            send_sem=sib_s.at[which, p], recv_sem=sib_r.at[which, p],
            device_id=sib, device_id_type=MESH)
        copy.start()
        return copy

    def add(p, fixed, other):
        here = cut(ps, p, fixed, (1,))
        here[...] = (here[...].astype(F32) + other.astype(F32)).astype(BF)

    sibs = {}
    sends = {}

    def send(p, s):
        d = (p + s) % 6
        fixed = {(p + k) % 6: bits[(p + k) % 6] for k in range(s)}
        fixed[d] = 1 - bits[d]
        free = 5 - s
        copy = pltpu.make_async_remote_copy(
            src_ref=cut(ps, p, fixed, (1,)),
            dst_ref=rs[s].at[(slice(None),) * free + (slice(None), pl.ds(OUT_AT[p], OUT_W[p]))],
            send_sem=st_s.at[s, p], recv_sem=st_r.at[s, p],
            device_id=partner(x, y, z, c, d), device_id_type=MESH)
        copy.start()
        sends[p, s] = copy

    for p in range(6):
        sibs[0, p] = product(p, 0)
        if p:
            q = p - 1
            sibs[0, q].wait_recv()
            f = {q: 1 - bits[q]}
            add(q, f, cut(rb, q, f)[...])
            send(q, 0)
    q = 5
    sibs[0, q].wait_recv()
    f = {q: 1 - bits[q]}
    add(q, f, cut(rb, q, f)[...])
    send(q, 0)
    for p in range(6):
        sibs[1, p] = product(p, 1)
    for p in range(6):
        sibs[1, p].wait_recv()
        f = {p: bits[p]}
        add(p, f, cut(rb, p, f)[...])
    for s in range(6):
        for p in range(6):
            sends[p, s].wait_recv()
            fixed = {(p + k) % 6: bits[(p + k) % 6] for k in range(s + 1)}
            add(p, fixed, rs[s][(slice(None),) * (5 - s) + (slice(None), pl.ds(OUT_AT[p], OUT_W[p]))])
            if s < 5:
                send(p, s + 1)
    me = ps.at[(1,) + tuple(bits)]
    last = pltpu.make_async_remote_copy(
        src_ref=me, dst_ref=fin.at[0], send_sem=sib_s.at[0, 6], recv_sem=sib_r.at[0, 6],
        device_id=sib, device_id_type=MESH)
    last.start()
    out[c] = me[...]
    last.wait_recv()
    out[1 - c] = fin[0]
    last.wait_send()
    for p in range(6):
        sibs[0, p].wait_send()
        sibs[1, p].wait_send()
        for s in range(6):
            sends[p, s].wait_send()


def moe_out(act, down, cid):
    cube = (2,) * 6
    return pl.pallas_call(
        moe_out_kernel,
        out_shape=jax.ShapeDtypeStruct((2, 16, 3584), BF),
        in_specs=[pl.BlockSpec(memory_space=pltpu.VMEM)] * 2,
        out_specs=pl.BlockSpec(memory_space=pltpu.VMEM),
        scratch_shapes=[
            pltpu.VMEM((2,) + cube + (16, 3584), BF),
            pltpu.VMEM(cube + (16, 3584), BF),
        ] + [pltpu.VMEM((2,) * (5 - s) + (16, 3584), BF) for s in range(6)] + [
            pltpu.SemaphoreType.DMA((2, 7)), pltpu.SemaphoreType.DMA((2, 7)),
            pltpu.SemaphoreType.DMA((6, 6)), pltpu.SemaphoreType.DMA((6, 6)),
            pltpu.VMEM((1, 16, 3584), BF),
        ],
        compiler_params=pltpu.CompilerParams(collective_id=cid, has_side_effects=True, vmem_limit_bytes=56 << 20),
        cost_estimate=pl.CostEstimate(flops=2 * 1024 * 256 * 7168, bytes_accessed=1 << 23, transcendentals=0),
    )(act.reshape(cube + (16, 256)), down)


ROW_AT = (0, 80, 160, 0, 80, 160)
ROW_N = (80, 80, 64, 80, 80, 64)


def moe_in_kernel(hid, sq, gate, up, act, own, buf, sqb, rows, accg, accu, st_s, st_r, sb_s, sb_r):
    x, y, z, c = place()
    bits = cube_bits(x, y, z)
    yh, yl, xh, xl, zh, zl = bits
    meet(range(7), x, y, z, c)
    sib = partner(x, y, z, c, SIBLING)

    def cut(p, known):
        g = lambda d: slice(None) if d in known else bits[d]
        if p == 6:
            return sqb.at[g(0), g(1), g(2), g(3), g(4), g(5), c]
        return buf.at[g(2), g(3), g(0), g(1), p // 3, g(4), g(5), c, pl.ds(ROW_AT[p], ROW_N[p]), :]

    def fresh(p, s):
        first = 2 if p == 6 else p
        known = [(first + k) % 6 for k in range(max(s - 1, 0))]
        if s == 0:
            return cut(p, [])
        d = (first + s - 1) % 6
        g = lambda e: slice(None) if e in known else (1 - bits[e] if e == d else bits[e])
        if p == 6:
            return sqb.at[g(0), g(1), g(2), g(3), g(4), g(5), c]
        return buf.at[g(2), g(3), g(0), g(1), p // 3, g(4), g(5), c, pl.ds(ROW_AT[p], ROW_N[p]), :]

    buf[xh, xl, yh, yl, 0, zh, zl, c] = hid[0]
    buf[xh, xl, yh, yl, 1, zh, zl, c] = hid[1]
    sqb[yh, yl, xh, xl, zh, zl, c] = sq[...]
    sends, sibs = {}, {}
    for s in range(7):
        for p in range(7):
            first = 2 if p == 6 else p
            if s:
                sends[p, s - 1].wait_recv()
            if s < 6:
                here = cut(p, [(first + k) % 6 for k in range(s)])
                copy = pltpu.make_async_remote_copy(
                    src_ref=here, dst_ref=here, send_sem=st_s.at[s, p], recv_sem=st_r.at[s, p],
                    device_id=partner(x, y, z, c, (first + s) % 6), device_id_type=MESH)
                copy.start()
                sends[p, s] = copy
            here = fresh(p, s)
            copy = pltpu.make_async_remote_copy(
                src_ref=here, dst_ref=here, send_sem=sb_s.at[s, p], recv_sem=sb_r.at[s, p],
                device_id=sib, device_id_type=MESH)
            copy.start()
            sibs[p, s] = copy
    for s in range(7):
        for p in range(7):
            sibs[p, s].wait_recv()

    for j in range(4):
        ax = j if j < 2 else 5 - j
        for t in range(4):
            for h in range(2):
                at = t * 256 + h * 128
                rows[at:at + 128, :] = buf[j // 2, j % 2, t // 2, t % 2, h].reshape(1792, 128).T

        spot = (yh * 2 + yl) * 256 + (xh * 2 + xl) * 64 + (zh * 2 + zl) * 16
        own[j] = rows[pl.ds(pl.multiple_of(spot, 16), 16), :]
        for k, (w, acc) in enumerate(((gate, accg), (up, accu))):
            v = jnp.concatenate([w[ax, 0], w[ax, 1], w[ax, 3], w[ax, 2]], axis=0)
            got = jnp.dot(rows[...], v, preferred_element_type=F32)
            if j:
                acc[...] += got
            else:
                acc[...] = got
    lane = lax.broadcasted_iota(jnp.int32, (256, 128), 1)
    token = lax.broadcasted_iota(jnp.int32, (256, 128), 0) // 8
    for t in range(4):
        info = sqb[t // 2, t % 2].reshape(32, 8, 128)
        total = jnp.broadcast_to(jnp.sum(info, axis=0)[None], (32, 8, 128)).reshape(256, 128)
        total = jnp.sum(jnp.where(lane == token + 32, total, 0.0), axis=1, keepdims=True)
        mine = (x * 4 + z) * 2 + c
        wt = jnp.sum(jnp.where(lane == mine, info.reshape(256, 128), 0.0), axis=1, keepdims=True)
        scale = lax.rsqrt(total / 7168.0 + 1e-6)
        at = t * 256
        g = accg[at:at + 256, :] * scale
        u = accu[at:at + 256, :] * scale
        act[at:at + 256, :] = (g * u / (1.0 + jnp.exp(-g)) * wt).astype(BF)
    for s in range(7):
        for p in range(7):
            sibs[p, s].wait_send()
            if s < 6:
                sends[p, s].wait_send()


def moe_in(hid, sq, gate, up, cid):
    cube = (2,) * 6
    return pl.pallas_call(
        moe_in_kernel,
        out_shape=(jax.ShapeDtypeStruct((1024, 256), BF), jax.ShapeDtypeStruct((4, 16, 1792), BF)),
        in_specs=[pl.BlockSpec(memory_space=pltpu.VMEM)] * 4,
        out_specs=(pl.BlockSpec(memory_space=pltpu.VMEM),) * 2,
        scratch_shapes=[
            pltpu.VMEM((2, 2, 2, 2, 2, 2, 2, 2, 224, 128), BF),
            pltpu.VMEM((2, 2, 2, 2, 2, 2, 2, 8, 128), F32),
            pltpu.VMEM((1024, 1792), BF),
            pltpu.VMEM((1024, 256), F32),
            pltpu.VMEM((1024, 256), F32),
            pltpu.SemaphoreType.DMA((6, 7)), pltpu.SemaphoreType.DMA((6, 7)),
            pltpu.SemaphoreType.DMA((7, 7)), pltpu.SemaphoreType.DMA((7, 7)),
        ],
        compiler_params=pltpu.CompilerParams(collective_id=cid, has_side_effects=True, vmem_limit_bytes=56 << 20),
        cost_estimate=pl.CostEstimate(flops=2 * 1024 * 512 * 7168, bytes_accessed=1 << 23, transcendentals=0),
    )(hid, sq, gate.reshape(4, 4, 448, 256), up.reshape(4, 4, 448, 256))


def gray_swap(a, axis):
    parts = [lax.slice_in_dim(a, i, i + 1, axis=axis) for i in (0, 1, 3, 2)]
    return jnp.concatenate(parts, axis=axis)


def per_device(
    query_nope,
    query_rope,
    key_absorb,
    latent_cache,
    new_latent,
    context_lengths,
    value_absorb,
    out_proj,
    residual,
    norm_gain,
    routes,
    gate_weights,
    expert_gate,
    expert_up,
    expert_down,
):
    expert_count = lax.axis_size("expert")
    tensor_count = lax.axis_size("tensor")
    local_heads = key_absorb.shape[0]
    nope_dim = key_absorb.shape[1]
    latent_dim = key_absorb.shape[2]
    rope_dim = query_rope.shape[1] // local_heads
    group_rows = query_nope.shape[0]
    requests = latent_cache.shape[0]
    context = latent_cache.shape[1]
    nope_query = query_nope.reshape(group_rows, local_heads, nope_dim)
    absorbed = jnp.einsum(
        "rhn,hnl->rhl", nope_query, key_absorb, preferred_element_type=jnp.float32
    ).astype(jnp.bfloat16)
    rope_query = query_rope.reshape(group_rows, local_heads, rope_dim)
    absorbed, rope_query = (
        lax.all_to_all(absorbed, "tensor", split_axis=0, concat_axis=1, tiled=True),
        lax.all_to_all(rope_query, "tensor", split_axis=0, concat_axis=1, tiled=True),
    )
    queries = jnp.concatenate([absorbed, rope_query], axis=2)
    score_scale = 1.0 / math.sqrt(nope_dim + rope_dim)
    scores = (
        jnp.einsum("rhc,rpc->rhp", queries, latent_cache, preferred_element_type=jnp.float32)
        * score_scale
    )
    own_score = (
        jnp.einsum("rhc,rc->rh", queries, new_latent, preferred_element_type=jnp.float32)
        * score_scale
    )
    in_range = lax.broadcasted_iota(jnp.int32, (requests, context), 1) < context_lengths[:, None]
    scores = jnp.where(in_range[:, None, :], scores, -jnp.inf)
    row_max = jnp.maximum(jnp.max(scores, axis=2), own_score)
    exp_scores = jnp.exp(scores - row_max[:, :, None])
    own_expo = jnp.exp(own_score - row_max)
    denom_sum = jnp.sum(exp_scores, axis=2) + own_expo
    weights = (exp_scores / denom_sum[:, :, None]).astype(jnp.bfloat16)
    own_weight = (own_expo / denom_sum).astype(jnp.bfloat16)
    attended = jnp.einsum(
        "rhp,rpl->rhl", weights, latent_cache[:, :, :latent_dim], preferred_element_type=jnp.float32
    )
    attended = attended + own_weight.astype(jnp.float32)[:, :, None] * new_latent[
        :, None, :latent_dim
    ].astype(jnp.float32)
    attended = attended.astype(jnp.bfloat16)
    attended = lax.all_to_all(attended, "tensor", split_axis=1, concat_axis=0, tiled=True)
    head_out = jnp.einsum(
        "rhl,hlv->rhv", attended, value_absorb, preferred_element_type=jnp.float32
    ).astype(jnp.bfloat16)
    head_out = head_out.reshape(group_rows, -1)
    partial_value = jnp.dot(
        lax.all_gather(head_out, "expert", axis=0, tiled=True),
        out_proj,
        preferred_element_type=jnp.float32,
    )
    local_width = out_proj.shape[1]
    partial_value = partial_value.astype(jnp.bfloat16).reshape(
        4, 4, 2, tensor_count, requests, local_width
    )
    partial_value = gray_swap(gray_swap(partial_value, 0), 1)
    partial_value = jnp.transpose(partial_value, (3, 0, 1, 2, 4, 5)).reshape(-1, local_width)
    attn_block = lax.psum_scatter(partial_value, "tensor", scatter_dimension=0, tiled=True)
    residual_block = lax.all_to_all(
        residual.reshape(requests, expert_count, local_width), "expert", 1, 0, tiled=True
    ).reshape(4, 4, -1, local_width)
    residual_block = gray_swap(gray_swap(residual_block, 0), 1).reshape(-1, local_width)
    hidden = residual_block.astype(F32) + attn_block.astype(F32)
    squares = jnp.sum(hidden * hidden, axis=1)
    gain = lax.dynamic_slice_in_dim(
        norm_gain, lax.axis_index("expert") * local_width, local_width, 0
    )
    block = (hidden * gain.astype(F32)[None, :]).astype(BF)
    block = jnp.swapaxes(block.reshape(2, -1, local_width), 1, 2)
    experts = lax.broadcasted_iota(jnp.int32, (1, 1, expert_count), 2)
    table = jnp.sum(
        jnp.where(routes[:, :, None] == experts, gate_weights[:, :, None], 0.0), axis=1
    )
    side = jnp.concatenate(
        [table, jnp.swapaxes(squares.reshape(expert_count, requests), 0, 1),
         jnp.zeros((requests, 64), F32)], axis=1)
    act, own = moe_in(block, side, expert_gate, expert_up, 1)
    routed = moe_out(act, expert_down[0], 2)
    core = lax.axis_index("expert") % 2
    routed = lax.dynamic_slice_in_dim(routed, core * requests, requests, 1)
    routed = jnp.swapaxes(routed, 0, 1).reshape(requests, -1)
    own = lax.dynamic_slice_in_dim(own, core * requests, requests, 1)
    own = gray_swap(gray_swap(own.reshape(4, requests, 4, 448), 0), 2)
    own = jnp.swapaxes(own, 0, 1).reshape(requests, -1)
    hidden = own.astype(F32) / norm_gain.astype(F32)[None, :]
    return (hidden + routed.astype(F32)).astype(BF)


def solution(mesh):
    placed = (
        P("expert", "tensor"),
        P("expert", "tensor"),
        P("tensor", None, None),
        P(("expert", "tensor"), None, None),
        P(("expert", "tensor"), None),
        P(("expert", "tensor")),
        P("tensor", None, None),
        P("tensor", "expert"),
        P(("expert", "tensor"), None),
        P(),
        P(("expert", "tensor"), None),
        P(("expert", "tensor"), None),
        P("expert", None, "tensor"),
        P("expert", None, "tensor"),
        P("expert", "tensor", None),
    )
    return jax.shard_map(
        per_device,
        mesh=mesh,
        in_specs=placed,
        out_specs=P(("expert", "tensor"), None),
        check_vma=False,
    )
```

```python
import functools, math
import jax, jax.numpy as jnp
from jax import lax
from jax.experimental import pallas as pl
from jax.experimental.pallas import tpu as pltpu
from jax.sharding import PartitionSpec as P

MESH = pl.DeviceIdType.MESH
BF = jnp.bfloat16
F32 = jnp.float32
SIBLING = 6


def place():
    e, y = lax.axis_index("expert"), lax.axis_index("tensor")
    return e // 8, y, (e // 2) % 4, e % 2


def cube_bits(x, y, z):
    out = []
    for v in (y, x, z):
        g = jnp.where(v >= 2, 5 - v, v)
        out += [g // 2, g % 2]
    return out


def partner(x, y, z, c, d):
    if d == SIBLING:
        return ((x * 4 + z) * 2 + 1 - c, y)
    at = [y, x, z]
    v = at[d // 2]
    at[d // 2] = 3 - v if d % 2 == 0 else v + 1 - 2 * (v % 2)
    y, x, z = at
    return ((x * 4 + z) * 2 + c, y)


def meet(dims, x, y, z, c):
    barrier = pltpu.get_barrier_semaphore()
    for d in dims:
        pl.semaphore_signal(barrier, inc=1, device_id=partner(x, y, z, c, d), device_id_type=MESH)
    pl.semaphore_wait(barrier, len(dims))


OUT_W = (640, 640, 640, 640, 512, 512)
OUT_AT = (0, 640, 1280, 1920, 2560, 3072)


def moe_out_kernel(act, down, out, ps, rb, r0, r1, r2, r3, r4, r5, sib_s, sib_r, st_s, st_r, fin):
    x, y, z, c = place()
    bits = cube_bits(x, y, z)
    rs = (r0, r1, r2, r3, r4, r5)
    meet(range(7), x, y, z, c)
    sib = partner(x, y, z, c, SIBLING)

    def cut(ref, p, fixed, lead=()):
        idx = tuple(fixed[d] if d in fixed else slice(None) for d in range(6))
        return ref.at[lead + idx + (slice(None), pl.ds(OUT_AT[p], OUT_W[p]))]

    def product(p, which):
        b = 1 - bits[p] if which == 0 else bits[p]

        def one(side, carry):
            half = jnp.where(side == 0, 1 - c, c)
            rows = act[tuple(b if d == p else slice(None) for d in range(6))]
            rows = rows.reshape(512, 256)
            cols = pl.ds(pl.multiple_of(half * 3584 + OUT_AT[p], 128), OUT_W[p])
            got = jnp.dot(rows, down[:, cols], preferred_element_type=F32).astype(BF)
            cut(ps, p, {p: b}, (side,))[...] = got.reshape(2, 2, 2, 2, 2, 16, OUT_W[p])
            return carry

        lax.fori_loop(0, 2, one, 0)
        copy = pltpu.make_async_remote_copy(
            src_ref=cut(ps, p, {p: b}, (0,)), dst_ref=cut(rb, p, {p: b}),
            send_sem=sib_s.at[which, p], recv_sem=sib_r.at[which, p],
            device_id=sib, device_id_type=MESH)
        copy.start()
        return copy

    def add(p, fixed, other):
        here = cut(ps, p, fixed, (1,))
        here[...] = (here[...].astype(F32) + other.astype(F32)).astype(BF)

    sibs = {}
    sends = {}

    def send(p, s):
        d = (p + s) % 6
        fixed = {(p + k) % 6: bits[(p + k) % 6] for k in range(s)}
        fixed[d] = 1 - bits[d]
        free = 5 - s
        copy = pltpu.make_async_remote_copy(
            src_ref=cut(ps, p, fixed, (1,)),
            dst_ref=rs[s].at[(slice(None),) * free + (slice(None), pl.ds(OUT_AT[p], OUT_W[p]))],
            send_sem=st_s.at[s, p], recv_sem=st_r.at[s, p],
            device_id=partner(x, y, z, c, d), device_id_type=MESH)
        copy.start()
        sends[p, s] = copy

    for p in range(6):
        sibs[0, p] = product(p, 0)
        if p:
            q = p - 1
            sibs[0, q].wait_recv()
            f = {q: 1 - bits[q]}
            add(q, f, cut(rb, q, f)[...])
            send(q, 0)
    q = 5
    sibs[0, q].wait_recv()
    f = {q: 1 - bits[q]}
    add(q, f, cut(rb, q, f)[...])
    send(q, 0)
    for p in range(6):
        sibs[1, p] = product(p, 1)
    for p in range(6):
        sibs[1, p].wait_recv()
        f = {p: bits[p]}
        add(p, f, cut(rb, p, f)[...])
    for s in range(6):
        for p in range(6):
            sends[p, s].wait_recv()
            fixed = {(p + k) % 6: bits[(p + k) % 6] for k in range(s + 1)}
            add(p, fixed, rs[s][(slice(None),) * (5 - s) + (slice(None), pl.ds(OUT_AT[p], OUT_W[p]))])
            if s < 5:
                send(p, s + 1)
    me = ps.at[(1,) + tuple(bits)]
    last = pltpu.make_async_remote_copy(
        src_ref=me, dst_ref=fin.at[0], send_sem=sib_s.at[0, 6], recv_sem=sib_r.at[0, 6],
        device_id=sib, device_id_type=MESH)
    last.start()
    out[c] = me[...]
    last.wait_recv()
    out[1 - c] = fin[0]
    last.wait_send()
    for p in range(6):
        sibs[0, p].wait_send()
        sibs[1, p].wait_send()
        for s in range(6):
            sends[p, s].wait_send()


def moe_out(act, down, cid):
    cube = (2,) * 6
    return pl.pallas_call(
        moe_out_kernel,
        out_shape=jax.ShapeDtypeStruct((2, 16, 3584), BF),
        in_specs=[pl.BlockSpec(memory_space=pltpu.VMEM)] * 2,
        out_specs=pl.BlockSpec(memory_space=pltpu.VMEM),
        scratch_shapes=[
            pltpu.VMEM((2,) + cube + (16, 3584), BF),
            pltpu.VMEM(cube + (16, 3584), BF),
        ] + [pltpu.VMEM((2,) * (5 - s) + (16, 3584), BF) for s in range(6)] + [
            pltpu.SemaphoreType.DMA((2, 7)), pltpu.SemaphoreType.DMA((2, 7)),
            pltpu.SemaphoreType.DMA((6, 6)), pltpu.SemaphoreType.DMA((6, 6)),
            pltpu.VMEM((1, 16, 3584), BF),
        ],
        compiler_params=pltpu.CompilerParams(collective_id=cid, has_side_effects=True, vmem_limit_bytes=56 << 20),
        cost_estimate=pl.CostEstimate(flops=2 * 1024 * 256 * 7168, bytes_accessed=1 << 23, transcendentals=0),
    )(act.reshape(cube + (16, 256)), down)


ROW_AT = (0, 80, 160, 0, 80, 160)
ROW_N = (80, 80, 64, 80, 80, 64)


def middle_kernel(head, proj, res, gain, table, gate, up, act, own, heads, part, summed, turn, got,
                  buf, sqb, rows, accg, accu, h_s, h_r, hs_s, hs_r, y_s, y_r, t_s, t_r, st_s, st_r, sb_s, sb_r):
    x, y, z, c = place()
    bits = cube_bits(x, y, z)
    yh, yl, xh, xl, zh, zl = bits
    across = ((x * 4 + z) * 2 + c, (y + 2) % 4)
    barrier = pltpu.get_barrier_semaphore()
    for d in range(7):
        pl.semaphore_signal(barrier, inc=1, device_id=partner(x, y, z, c, d), device_id_type=MESH)
    pl.semaphore_signal(barrier, inc=1, device_id=across, device_id_type=MESH)
    pl.semaphore_wait(barrier, 8)
    sib = partner(x, y, z, c, SIBLING)

    def head_cut(p, free, flip=None):
        g = lambda d: slice(None) if d in free else (1 - bits[d] if d == flip else bits[d])
        return heads.at[g(2), g(3), g(4), g(5), c, :, pl.ds(p * 1024, 1024)]

    def around(p, k):
        return [2 + (p + i) % 4 for i in range(k)]

    def residual_turn(k):
        d = (SIBLING, 2, 3, 4, 5)[k]
        mine = c if d == SIBLING else bits[d]
        at = tuple(1 - mine if e == d else slice(None) for e in (2, 3, 4, 5, SIBLING))
        copy = pltpu.make_async_remote_copy(
            src_ref=turn.at[at], dst_ref=got.at[k], send_sem=t_s.at[k], recv_sem=t_r.at[k],
            device_id=partner(x, y, z, c, d), device_id_type=MESH)
        copy.start()
        return copy, at

    heads[xh, xl, zh, zl, c] = head[...]
    turn[...] = res[...]
    sends, sibs = {}, {}
    turning = None
    for s in range(5):
        for p in range(4):
            if s:
                sends[p, s - 1].wait_recv()
            if s < 4:
                here = head_cut(p, around(p, s))
                copy = pltpu.make_async_remote_copy(
                    src_ref=here, dst_ref=here, send_sem=h_s.at[s, p], recv_sem=h_r.at[s, p],
                    device_id=partner(x, y, z, c, 2 + (p + s) % 4), device_id_type=MESH)
                copy.start()
                sends[p, s] = copy
            here = head_cut(p, around(p, s - 1), 2 + (p + s - 1) % 4) if s else head_cut(p, [])
            copy = pltpu.make_async_remote_copy(
                src_ref=here, dst_ref=here, send_sem=hs_s.at[s, p], recv_sem=hs_r.at[s, p],
                device_id=sib, device_id_type=MESH)
            copy.start()
            sibs[p, s] = copy
        if turning is not None:
            turning[0].wait()
            turn[turning[1]] = got[s - 1]
        turning = residual_turn(s)
    for s in range(5):
        for p in range(4):
            sibs[p, s].wait_recv()
    for k in range(4):
        v = heads[k // 2, k % 2].reshape(256, 4096)
        v = jnp.dot(v, proj[...], preferred_element_type=F32).reshape(8, 4, 8, 224)
        for t in range(4):
            part[t, k] = v[:, t].reshape(64, 224).astype(BF)
    copies = []
    for k in range(1, 4):
        t = (y + k) % 4
        copy = pltpu.make_async_remote_copy(
            src_ref=part.at[t], dst_ref=summed.at[k - 1], send_sem=y_s.at[k - 1], recv_sem=y_r.at[k - 1],
            device_id=((x * 4 + z) * 2 + c, t), device_id_type=MESH)
        copy.start()
        copies.append(copy)
    turning[0].wait()
    turn[turning[1]] = got[4]
    total = part[y].astype(F32)
    for k in range(3):
        copies[k].wait_recv()
        total = total + summed[k].astype(F32)
    total = total.reshape(256, 224).astype(BF).astype(F32)
    hidden = total + turn[...].reshape(256, 256)[:, :224]
    squares = jnp.sum(hidden * hidden, axis=1, keepdims=True).reshape(32, 8, 1)
    lane3 = lax.broadcasted_iota(jnp.int32, (32, 8, 128), 2)
    from3 = lax.broadcasted_iota(jnp.int32, (32, 8, 128), 0)
    spread = jnp.sum(jnp.where(lane3 == from3 + 32, squares, 0.0), axis=0)
    sqb[yh, yl, xh, xl, zh, zl, c] = table[...] + spread
    hid = (hidden * gain[...]).T.astype(BF)
    buf[xh, xl, yh, yl, 0, zh, zl, c] = hid[:, :128]
    buf[xh, xl, yh, yl, 1, zh, zl, c] = hid[:, 128:]
    for s in range(5):
        for p in range(4):
            sibs[p, s].wait_send()
            if s < 4:
                sends[p, s].wait_send()
    for copy in copies:
        copy.wait_send()

    def cut(p, known):
        g = lambda d: slice(None) if d in known else bits[d]
        if p == 6:
            return sqb.at[g(0), g(1), g(2), g(3), g(4), g(5), c]
        return buf.at[g(2), g(3), g(0), g(1), p // 3, g(4), g(5), c, pl.ds(ROW_AT[p], ROW_N[p]), :]

    def fresh(p, s):
        first = 2 if p == 6 else p
        known = [(first + k) % 6 for k in range(max(s - 1, 0))]
        if s == 0:
            return cut(p, [])
        d = (first + s - 1) % 6
        g = lambda e: slice(None) if e in known else (1 - bits[e] if e == d else bits[e])
        if p == 6:
            return sqb.at[g(0), g(1), g(2), g(3), g(4), g(5), c]
        return buf.at[g(2), g(3), g(0), g(1), p // 3, g(4), g(5), c, pl.ds(ROW_AT[p], ROW_N[p]), :]

    sends, sibs = {}, {}
    for s in range(7):
        for p in range(7):
            first = 2 if p == 6 else p
            if s:
                sends[p, s - 1].wait_recv()
            if s < 6:
                here = cut(p, [(first + k) % 6 for k in range(s)])
                copy = pltpu.make_async_remote_copy(
                    src_ref=here, dst_ref=here, send_sem=st_s.at[s, p], recv_sem=st_r.at[s, p],
                    device_id=partner(x, y, z, c, (first + s) % 6), device_id_type=MESH)
                copy.start()
                sends[p, s] = copy
            here = fresh(p, s)
            copy = pltpu.make_async_remote_copy(
                src_ref=here, dst_ref=here, send_sem=sb_s.at[s, p], recv_sem=sb_r.at[s, p],
                device_id=sib, device_id_type=MESH)
            copy.start()
            sibs[p, s] = copy
    for s in range(7):
        for p in range(7):
            sibs[p, s].wait_recv()

    for j in range(4):
        ax = j if j < 2 else 5 - j
        for t in range(4):
            for h in range(2):
                at = t * 256 + h * 128
                rows[at:at + 128, :] = buf[j // 2, j % 2, t // 2, t % 2, h].reshape(1792, 128).T

        spot = (yh * 2 + yl) * 256 + (xh * 2 + xl) * 64 + (zh * 2 + zl) * 16
        own[j] = rows[pl.ds(pl.multiple_of(spot, 16), 16), :]
        for k, (w, acc) in enumerate(((gate, accg), (up, accu))):
            v = jnp.concatenate([w[ax, 0], w[ax, 1], w[ax, 3], w[ax, 2]], axis=0)
            got = jnp.dot(rows[...], v, preferred_element_type=F32)
            if j:
                acc[...] += got
            else:
                acc[...] = got
    lane = lax.broadcasted_iota(jnp.int32, (256, 128), 1)
    token = lax.broadcasted_iota(jnp.int32, (256, 128), 0) // 8
    for t in range(4):
        info = sqb[t // 2, t % 2].reshape(32, 8, 128)
        total = jnp.broadcast_to(jnp.sum(info, axis=0)[None], (32, 8, 128)).reshape(256, 128)
        total = jnp.sum(jnp.where(lane == token + 32, total, 0.0), axis=1, keepdims=True)
        mine = (x * 4 + z) * 2 + c
        wt = jnp.sum(jnp.where(lane == mine, info.reshape(256, 128), 0.0), axis=1, keepdims=True)
        scale = lax.rsqrt(total / 7168.0 + 1e-6)
        at = t * 256
        g = accg[at:at + 256, :] * scale
        u = accu[at:at + 256, :] * scale
        act[at:at + 256, :] = (g * u / (1.0 + jnp.exp(-g)) * wt).astype(BF)
    for s in range(7):
        for p in range(7):
            sibs[p, s].wait_send()
            if s < 6:
                sends[p, s].wait_send()


def middle(head, proj, res, gain, table, gate, up, cid):
    vm = lambda shape, kind=BF: pltpu.VMEM(shape, kind)
    dma = lambda *shape: pltpu.SemaphoreType.DMA(shape)
    two = lambda n: (2,) * n
    return pl.pallas_call(
        middle_kernel,
        out_shape=(jax.ShapeDtypeStruct((1024, 256), BF), jax.ShapeDtypeStruct((4, 16, 1792), BF)),
        in_specs=[pl.BlockSpec(memory_space=pltpu.VMEM)] * 7,
        out_specs=(pl.BlockSpec(memory_space=pltpu.VMEM),) * 2,
        scratch_shapes=[
            vm(two(5) + (32, 4096)), vm((4, 4, 64, 224)), vm((3, 4, 64, 224)),
            vm(two(5) + (8, 256), F32), vm((5,) + two(4) + (8, 256), F32),
            vm(two(8) + (224, 128)), vm(two(7) + (8, 128), F32),
            vm((1024, 1792)), vm((1024, 256), F32), vm((1024, 256), F32),
            dma(4, 4), dma(4, 4), dma(5, 4), dma(5, 4), dma(3), dma(3), dma(5), dma(5),
            dma(6, 7), dma(6, 7), dma(7, 7), dma(7, 7),
        ],
        compiler_params=pltpu.CompilerParams(
            collective_id=cid, has_side_effects=True, vmem_limit_bytes=60 << 20),
        cost_estimate=pl.CostEstimate(
            flops=2 * 1024 * 512 * 7168, bytes_accessed=1 << 23, transcendentals=1 << 18),
    )(head, proj, res, gain, table, gate.reshape(4, 4, 448, 256), up.reshape(4, 4, 448, 256))


def gray_swap(a, axis):
    parts = [lax.slice_in_dim(a, i, i + 1, axis=axis) for i in (0, 1, 3, 2)]
    return jnp.concatenate(parts, axis=axis)


def per_device(
    query_nope,
    query_rope,
    key_absorb,
    latent_cache,
    new_latent,
    context_lengths,
    value_absorb,
    out_proj,
    residual,
    norm_gain,
    routes,
    gate_weights,
    expert_gate,
    expert_up,
    expert_down,
):
    expert_count = lax.axis_size("expert")
    tensor_count = lax.axis_size("tensor")
    local_heads = key_absorb.shape[0]
    nope_dim = key_absorb.shape[1]
    latent_dim = key_absorb.shape[2]
    rope_dim = query_rope.shape[1] // local_heads
    group_rows = query_nope.shape[0]
    requests = latent_cache.shape[0]
    context = latent_cache.shape[1]
    nope_query = query_nope.reshape(group_rows, local_heads, nope_dim)
    absorbed = jnp.einsum(
        "rhn,hnl->rhl", nope_query, key_absorb, preferred_element_type=jnp.float32
    ).astype(jnp.bfloat16)
    rope_query = query_rope.reshape(group_rows, local_heads, rope_dim)
    absorbed, rope_query = (
        lax.all_to_all(absorbed, "tensor", split_axis=0, concat_axis=1, tiled=True),
        lax.all_to_all(rope_query, "tensor", split_axis=0, concat_axis=1, tiled=True),
    )
    queries = jnp.concatenate([absorbed, rope_query], axis=2)
    score_scale = 1.0 / math.sqrt(nope_dim + rope_dim)
    scores = (
        jnp.einsum("rhc,rpc->rhp", queries, latent_cache, preferred_element_type=jnp.float32)
        * score_scale
    )
    own_score = (
        jnp.einsum("rhc,rc->rh", queries, new_latent, preferred_element_type=jnp.float32)
        * score_scale
    )
    in_range = lax.broadcasted_iota(jnp.int32, (requests, context), 1) < context_lengths[:, None]
    scores = jnp.where(in_range[:, None, :], scores, -jnp.inf)
    row_max = jnp.maximum(jnp.max(scores, axis=2), own_score)
    exp_scores = jnp.exp(scores - row_max[:, :, None])
    own_expo = jnp.exp(own_score - row_max)
    denom_sum = jnp.sum(exp_scores, axis=2) + own_expo
    weights = (exp_scores / denom_sum[:, :, None]).astype(jnp.bfloat16)
    own_weight = (own_expo / denom_sum).astype(jnp.bfloat16)
    attended = jnp.einsum(
        "rhp,rpl->rhl", weights, latent_cache[:, :, :latent_dim], preferred_element_type=jnp.float32
    )
    attended = attended + own_weight.astype(jnp.float32)[:, :, None] * new_latent[
        :, None, :latent_dim
    ].astype(jnp.float32)
    attended = attended.astype(jnp.bfloat16)
    attended = lax.all_to_all(attended, "tensor", split_axis=1, concat_axis=0, tiled=True)
    head_out = jnp.einsum(
        "rhl,hlv->rhv", attended, value_absorb, preferred_element_type=jnp.float32
    ).astype(jnp.bfloat16)
    head_out = head_out.reshape(group_rows, -1)
    requests, model_width = residual.shape
    local_width = out_proj.shape[1]
    blocks = jnp.pad(
        jnp.swapaxes(residual.reshape(requests, -1, local_width), 0, 1).astype(F32),
        ((0, 0), (0, 0), (0, 256 - local_width)),
    )
    blocks = gray_swap(gray_swap(blocks.reshape(4, 4, 2, requests, 256), 0), 1)
    blocks = blocks.reshape(2, 2, 2, 2, 2, requests, 256)
    gain = lax.dynamic_slice_in_dim(
        norm_gain, lax.axis_index("expert") * local_width, local_width, 0
    )
    gain = gain.astype(F32)[None, :]
    experts = lax.broadcasted_iota(jnp.int32, (1, 1, 128), 2)
    table = jnp.sum(
        jnp.where(routes[:, :, None] == experts, gate_weights[:, :, None], 0.0), axis=1
    )
    act, own = middle(head_out, out_proj, blocks, gain, table, expert_gate, expert_up, 1)
    routed = moe_out(act, expert_down[0], 2)
    core = lax.axis_index("expert") % 2
    routed = lax.dynamic_slice_in_dim(routed, core * requests, requests, 1)
    routed = jnp.swapaxes(routed, 0, 1).reshape(requests, -1)
    own = lax.dynamic_slice_in_dim(own, core * requests, requests, 1)
    own = gray_swap(gray_swap(own.reshape(4, requests, 4, 448), 0), 2)
    own = jnp.swapaxes(own, 0, 1).reshape(requests, -1)
    hidden = own.astype(F32) / norm_gain.astype(F32)[None, :]
    return (hidden + routed.astype(F32)).astype(BF)


def solution(mesh):
    placed = (
        P("expert", "tensor"),
        P("expert", "tensor"),
        P("tensor", None, None),
        P(("expert", "tensor"), None, None),
        P(("expert", "tensor"), None),
        P(("expert", "tensor")),
        P("tensor", None, None),
        P("tensor", "expert"),
        P(("expert", "tensor"), None),
        P(),
        P(("expert", "tensor"), None),
        P(("expert", "tensor"), None),
        P("expert", None, "tensor"),
        P("expert", None, "tensor"),
        P("expert", "tensor", None),
    )
    return jax.shard_map(
        per_device,
        mesh=mesh,
        in_specs=placed,
        out_specs=P(("expert", "tensor"), None),
        check_vma=False,
    )
```

```python
import functools, math
import jax, jax.numpy as jnp
from jax import lax
from jax.experimental import pallas as pl
from jax.experimental.pallas import tpu as pltpu
from jax.sharding import PartitionSpec as P

MESH = pl.DeviceIdType.MESH
BF = jnp.bfloat16
F32 = jnp.float32
SIBLING = 6


def place():
    e, y = lax.axis_index("expert"), lax.axis_index("tensor")
    return e // 8, y, (e // 2) % 4, e % 2


def cube_bits(x, y, z):
    out = []
    for v in (y, x, z):
        g = jnp.where(v >= 2, 5 - v, v)
        out += [g // 2, g % 2]
    return out


def partner(x, y, z, c, d):
    if d == SIBLING:
        return ((x * 4 + z) * 2 + 1 - c, y)
    at = [y, x, z]
    v = at[d // 2]
    at[d // 2] = 3 - v if d % 2 == 0 else v + 1 - 2 * (v % 2)
    y, x, z = at
    return ((x * 4 + z) * 2 + c, y)


def meet(dims, x, y, z, c):
    barrier = pltpu.get_barrier_semaphore()
    for d in dims:
        pl.semaphore_signal(barrier, inc=1, device_id=partner(x, y, z, c, d), device_id_type=MESH)
    pl.semaphore_wait(barrier, len(dims))


FREE, OTHER, MINE = "free", "other", "mine"


def index_of(bits, spec):
    return [slice(None) if spec.get(d) == FREE else (1 - bits[d] if spec.get(d) == OTHER else bits[d])
            for d in range(6)]


class Gather:
    def __init__(self, order, cut, send_sem, recv_sem, where, split=True):
        self.order, self.cut, self.where, self.split = order, cut, where, split
        self.sems = send_sem, recv_sem
        self.copies = {}

    def send(self, s, part):
        o = self.order
        spec = {d: FREE for d in o[:max(s - 1, 0) if self.split else s]}
        if part:
            spec[o[s - 1]] = OTHER
        ref = self.cut(spec)
        copy = pltpu.make_async_remote_copy(
            src_ref=ref, dst_ref=ref, send_sem=self.sems[0].at[s, part], recv_sem=self.sems[1].at[s, part],
            device_id=partner(*self.where, o[s]), device_id_type=MESH)
        copy.start()
        self.copies[s, part] = copy

    def last(self, part):
        o = self.order
        spec = {d: FREE for d in o[:-2]}
        spec[o[-1]] = OTHER
        if part:
            spec[o[-2]] = OTHER
        return spec

    def turn(self, s):
        if s == 0:
            self.send(0, 0)
            if self.split:
                self.send(1, 0)
            return
        for part in (0, 1) if self.split and s > 1 else (0,):
            self.copies[s - 1, part].wait_recv()
        if s < len(self.order):
            if self.split:
                self.send(s, 1)
                if s + 1 < len(self.order):
                    self.send(s + 1, 0)
            else:
                self.send(s, 0)

    def finish(self, part):
        self.copies[len(self.order) - 1, part].wait_recv()

    def wait_sends(self):
        for copy in self.copies.values():
            copy.wait_send()


ROW_AT = (0, 80, 160, 240, 320, 384)
ROW_N = (80, 80, 80, 80, 64, 64)


def middle_kernel(head, proj_hbm, proj2_hbm, res, gains, routes, weights, gate_hbm, up_hbm, gate2_hbm, up2_hbm,
                  act, own, proj, wts, heads, part, summed, gainf, turn, got, buf, sqb, acc, loads,
                  h_s, h_r, y_s, y_r, t_s, t_r, st_s, st_r):
    x, y, z, c = where = place()
    bits = cube_bits(x, y, z)
    yh, yl, xh, xl, zh, zl = bits
    chip = (x * 4 + z) * 2
    across = (chip + c, (y + 2) % 4)
    fetch = [pltpu.make_async_copy(a, b, loads.at[n]) for n, (a, b) in enumerate((
        (proj_hbm, proj.at[c]), (proj2_hbm, proj.at[1 - c]), (gate_hbm, wts.at[0, 0]), (up_hbm, wts.at[0, 1]),
        (gate2_hbm, wts.at[1, 0]), (up2_hbm, wts.at[1, 1])))]
    for copy in fetch:
        copy.start()
    barrier = pltpu.get_barrier_semaphore()
    for d in range(6):
        pl.semaphore_signal(barrier, inc=1, device_id=partner(x, y, z, c, d), device_id_type=MESH)
    pl.semaphore_signal(barrier, inc=1, device_id=across, device_id_type=MESH)
    heads[xh, xl, zh, zl] = head[...]
    for k in range(16):
        sx, sz = k // 4 ^ k // 8, k % 4 ^ k % 4 // 2
        v = [res[:, e * 224:(e + 1) * 224].astype(F32) for e in (2 * k, 2 * k + 1)]
        turn[sx // 2, sx % 2, sz // 2, sz % 2] = jnp.concatenate(v, axis=0).astype(BF)
    gainf[...] = gains[...].astype(F32)
    lane = lax.broadcasted_iota(jnp.int32, (8, 128), 1)
    table = jnp.zeros((8, 128), F32)
    for k in range(8):
        table = table + jnp.where(lane == routes[:, k:k + 1], weights[:, k:k + 1], 0.0)
    acc[...] = jnp.zeros_like(acc)
    pl.semaphore_wait(barrier, 7)

    def head_cut(p):
        def cut(spec):
            g = index_of(bits, spec)
            return heads.at[g[2], g[3], g[4], g[5], :, pl.ds(p * 1024, 1024)]
        return cut

    first = [Gather([2 + (p + i) % 4 for i in range(4)], head_cut(p), h_s.at[p], h_r.at[p], where) for p in range(4)]

    def residual_turn(k):
        d = 2 + k
        at = tuple(1 - bits[d] if e == d else slice(None) for e in (2, 3, 4, 5))
        copy = pltpu.make_async_remote_copy(
            src_ref=turn.at[at], dst_ref=got.at[k], send_sem=t_s.at[k], recv_sem=t_r.at[k],
            device_id=partner(x, y, z, c, d), device_id_type=MESH)
        copy.start()
        return copy, at

    turning = None
    for s in range(4):
        for g in first:
            g.turn(s)
        if turning is not None:
            turning[0].wait()
            turn[turning[1]] = got[s - 1]
        turning = residual_turn(s)
    for copy in fetch[:2]:
        copy.wait()
    for half in range(2):
        for g in first:
            g.finish(half)
    for k in range(2):
        v = heads[k].reshape(256, 4096)
        for n in range(2):
            o = lax.dot_general(v, proj[n], (((1,), (1,)), ((), ())), preferred_element_type=F32)
            o = o.reshape(8, 4, 8, 224)
            for t in range(4):
                part[t, n, k] = o[:, t].reshape(64, 224).astype(BF)
    copies = []
    for k in range(1, 4):
        t = (y + k) % 4
        copy = pltpu.make_async_remote_copy(
            src_ref=part.at[t], dst_ref=summed.at[k - 1], send_sem=y_s.at[k - 1], recv_sem=y_r.at[k - 1],
            device_id=(chip + c, t), device_id_type=MESH)
        copy.start()
        copies.append(copy)
    turning[0].wait()
    turn[turning[1]] = got[3]
    total = part[y].astype(F32)
    for k in range(3):
        copies[k].wait_recv()
        total = total + summed[k].astype(F32)
    total = total.astype(BF).astype(F32).reshape(2, 128, 224)
    residual = turn[...].astype(F32).reshape(16, 2, 8, 224)
    squares, hid = 0.0, []
    for n in range(2):
        hidden = total[n] + residual[:, n].reshape(128, 224)
        squares = squares + jnp.sum(hidden * hidden, axis=1, keepdims=True)
        hid.append((hidden * gainf[pl.ds(chip + n, 1), :]).T)
    lane3 = lax.broadcasted_iota(jnp.int32, (16, 8, 128), 2)
    from3 = lax.broadcasted_iota(jnp.int32, (16, 8, 128), 0)
    spread = jnp.sum(jnp.where(lane3 == from3 + 32, squares.reshape(16, 8, 1), 0.0), axis=0)
    sqb[yh, yl, xh, xl, zh, zl] = table + spread
    buf[xh, xl, yh, yl, zh, zl] = jnp.concatenate(hid, axis=0).astype(BF)

    def cut_of(p):
        def cut(spec):
            g = index_of(bits, spec)
            if p == 6:
                return sqb.at[g[0], g[1], g[2], g[3], g[4], g[5]]
            return buf.at[g[2], g[3], g[0], g[1], g[4], g[5], pl.ds(ROW_AT[p], ROW_N[p]), :]
        return cut

    def order_of(p):
        return [((4 if p == 6 else p) + k) % 6 for k in range(6)]

    second = [Gather(order_of(p), cut_of(p), st_s.at[p], st_r.at[p], where, p < 6) for p in range(7)]

    def work(p, spec):
        rows = pl.ds(ROW_AT[p], ROW_N[p])
        opts = [(0, 1) if spec.get(d) == FREE else ((1 - bits[d],) if spec.get(d) == OTHER else (bits[d],))
                for d in range(6)]
        inner = [(i, j, k, l) for i in opts[2] for j in opts[3] for k in opts[4] for l in opts[5]]
        outer = [(a, b) for a in opts[0] for b in opts[1]]
        lhs = []
        for a, b in outer:
            slab = [buf[i, j, a, b, k, l, rows, :] for i, j, k, l in inner]
            lhs.append(jnp.concatenate(slab, axis=0).T)
        lhs = jnp.concatenate(lhs, axis=0)
        for n in range(2):
            for m in range(2):
                v = [wts[n, m, 2 * i + (i + j - 2 * i * j), 2 * k + (k + l - 2 * k * l), rows, :]
                     for i, j, k, l in inner]
                o = jnp.dot(lhs, jnp.concatenate(v, axis=0), preferred_element_type=F32)
                for q, (a, b) in enumerate(outer):
                    acc[n, m, a, b] += o[q * 128:(q + 1) * 128]

    for s in range(6):
        for g in second:
            g.turn(s)
    for copy in fetch[2:]:
        copy.wait()
    for p in range(6):
        work(p, {d: FREE for d in order_of(p)[:5]})
    second[6].turn(6)
    for half in range(2):
        for p in range(6):
            second[p].finish(half)
            work(p, second[p].last(half))

    lane = lax.broadcasted_iota(jnp.int32, (128, 128), 1)
    token = lax.broadcasted_iota(jnp.int32, (128, 128), 0) // 8
    for t in range(4):
        info = sqb[t // 2, t % 2].reshape(16, 8, 128)
        total = jnp.broadcast_to(jnp.sum(info, axis=0)[None], (16, 8, 128)).reshape(128, 128)
        total = jnp.sum(jnp.where(lane == token + 32, total, 0.0), axis=1, keepdims=True)
        scale = lax.rsqrt(total / 7168.0 + 1e-6)
        for n in range(2):
            expert = chip + (c if n == 0 else 1 - c)
            wt = jnp.sum(jnp.where(lane == expert, info.reshape(128, 128), 0.0), axis=1, keepdims=True)
            g = acc[n, 0, t // 2, t % 2] * scale
            u = acc[n, 1, t // 2, t % 2] * scale
            act[t * 128:(t + 1) * 128, n * 256:(n + 1) * 256] = g * u / (1.0 + jnp.exp(-g)) * wt
    spot = (xh * 2 + xl) * 32 + (zh * 2 + zl) * 8
    row = lax.broadcasted_iota(jnp.int32, (16, 128), 0)
    pick = (lax.broadcasted_iota(jnp.int32, (16, 128), 1) == row + spot) & (row < 8)
    pick = jnp.where(pick, 1.0, 0.0).astype(BF)
    for j in range(4):
        v = jnp.concatenate([buf[j // 2, j % 2, yh, yl, k // 2, k % 2] for k in (0, 1, 3, 2)], axis=0)
        v = lax.dot_general(pick, v, (((1,), (1,)), ((), ())), preferred_element_type=F32)
        ax = j if j < 2 else 5 - j
        own[:, ax * 1792:(ax + 1) * 1792] = v.astype(BF)
    for g in first + second:
        g.wait_sends()
    for copy in copies:
        copy.wait_send()


def middle(head, proj, proj2, res, gains, routes, weights, gates, cid):
    vm = lambda shape, kind=BF: pltpu.VMEM(shape, kind)
    dma = lambda *shape: pltpu.SemaphoreType.DMA(shape)
    two = lambda n: (2,) * n
    inside = pl.BlockSpec(memory_space=pltpu.VMEM)
    outside = pl.BlockSpec(memory_space=pl.ANY)
    return pl.pallas_call(
        middle_kernel,
        out_shape=(jax.ShapeDtypeStruct((512, 512), F32), jax.ShapeDtypeStruct((16, 7168), BF)),
        in_specs=[inside, outside, outside] + [inside] * 4 + [outside] * 4,
        out_specs=(inside, inside),
        scratch_shapes=[
            vm((2, 224, 4096)), vm((2, 2, 4, 4, 448, 256)),
            vm(two(4) + (32, 4096)), vm((4, 2, 2, 64, 224)), vm((3, 2, 2, 64, 224)),
            vm((32, 224), F32), vm(two(4) + (16, 224)), vm((4,) + two(3) + (16, 224)),
            vm(two(6) + (448, 128)), vm(two(6) + (8, 128), F32), vm((2, 2, 2, 2, 128, 256), F32),
            dma(6), dma(4, 4, 2), dma(4, 4, 2), dma(3), dma(3), dma(4), dma(4), dma(7, 6, 2), dma(7, 6, 2),
        ],
        compiler_params=pltpu.CompilerParams(
            collective_id=cid, has_side_effects=True, vmem_limit_bytes=56 << 20),
        cost_estimate=pl.CostEstimate(
            flops=2 * 1024 * 512 * 7168, bytes_accessed=1 << 23, transcendentals=1 << 18),
    )(head, proj, proj2, res, gains, routes, weights, *[g.reshape(4, 4, 448, 256) for g in gates])


OUT_W = (640, 640, 640, 640, 512, 512)
OUT_AT = (0, 640, 1280, 1920, 2560, 3072)


def moe_out_kernel(act, down_hbm, others_hbm, out, down, ps, r0, r1, r2, r3, r4, r5, loads, st_s, st_r):
    x, y, z, c = place()
    bits = cube_bits(x, y, z)
    rs = (r0, r1, r2, r3, r4, r5)
    fetch = [
        pltpu.make_async_copy(down_hbm, down.at[pl.ds(0, 256)], loads.at[0]),
        pltpu.make_async_copy(others_hbm, down.at[pl.ds(256, 256)], loads.at[1]),
    ]
    for copy in fetch:
        copy.start()
    meet(range(6), x, y, z, c)

    def cut(ref, p, spec):
        idx = tuple(bits[d] if spec[d] == MINE else (1 - bits[d] if spec[d] == OTHER else slice(None))
                    for d in range(6) if d in spec)
        return ref.at[idx + (slice(None), pl.ds(OUT_AT[p], OUT_W[p]))]

    def spec_of(p, s, which):
        spec = {d: FREE for d in range(6)}
        for k in range(s):
            spec[(p + k) % 6] = MINE
        spec[(p + s) % 6] = OTHER
        if s < 5:
            spec[(p + s + 1) % 6] = OTHER if which == 0 else MINE
        return spec

    def product(p, spec):
        rows = act[tuple(bits[d] if spec[d] == MINE else (1 - bits[d] if spec[d] == OTHER else slice(None))
                         for d in range(6))]
        free = sum(spec[d] == FREE for d in range(6))
        rows = rows.reshape(8 << free, 512).astype(BF)
        halves = []
        for at in (OUT_AT[p], 3584 + OUT_AT[p]):
            o = jnp.dot(rows, down[:, at:at + OUT_W[p]], preferred_element_type=F32)
            halves.append(o.reshape(1 << free, 8, OUT_W[p]))
        got = jnp.concatenate(halves, axis=1).astype(BF)
        cut(ps, p, spec)[...] = got.reshape((2,) * free + (16, OUT_W[p]))

    sends = {}

    def landing(p, s, which):
        spec = spec_of(p, s, which)
        return cut(rs[s], p, {d: spec[d] for d in range(6) if d not in [(p + k) % 6 for k in range(s + 1)]})

    def send(p, s, which):
        copy = pltpu.make_async_remote_copy(
            src_ref=cut(ps, p, spec_of(p, s, which)), dst_ref=landing(p, s, which),
            send_sem=st_s.at[s, p, which], recv_sem=st_r.at[s, p, which],
            device_id=partner(x, y, z, c, (p + s) % 6), device_id_type=MESH)
        copy.start()
        sends[p, s, which] = copy

    def take(p, s, which):
        sends[p, s, which].wait_recv()
        spec = dict(spec_of(p, s, which))
        spec[(p + s) % 6] = MINE
        here, other = cut(ps, p, spec), landing(p, s, which)
        here[...] = (here[...].astype(F32) + other[...].astype(F32)).astype(BF)

    for copy in fetch:
        copy.wait()
    for which in (0, 1):
        for p in range(6):
            product(p, spec_of(p, 0, which))
            send(p, 0, which)
    for p in range(6):
        product(p, {d: MINE if d == p else FREE for d in range(6)})
    for s in range(5):
        for p in range(6):
            take(p, s, 0)
            send(p, s + 1, 0)
            if s < 4:
                send(p, s + 1, 1)
        for p in range(6):
            take(p, s, 1)
    for p in range(6):
        take(p, 5, 0)
    mine = ps[tuple(bits)].astype(F32)
    out[:, :3584] = mine[:8]
    out[:, 3584:] = mine[8:]
    for copy in sends.values():
        copy.wait_send()


def moe_out(act, down, others, cid):
    cube = (2,) * 6
    dma = lambda *shape: pltpu.SemaphoreType.DMA(shape)
    inside = pl.BlockSpec(memory_space=pltpu.VMEM)
    outside = pl.BlockSpec(memory_space=pl.ANY)
    return pl.pallas_call(
        moe_out_kernel,
        out_shape=jax.ShapeDtypeStruct((8, 7168), F32),
        in_specs=[inside, outside, outside],
        out_specs=inside,
        scratch_shapes=[
            pltpu.VMEM((512, 7168), BF),
            pltpu.VMEM(cube + (16, 3584), BF),
        ] + [pltpu.VMEM((2,) * (5 - s) + (16, 3584), BF) for s in range(6)] + [
            dma(2), dma(6, 6, 2), dma(6, 6, 2),
        ],
        compiler_params=pltpu.CompilerParams(
            collective_id=cid, has_side_effects=True, vmem_limit_bytes=56 << 20),
        cost_estimate=pl.CostEstimate(flops=2 * 1024 * 256 * 7168, bytes_accessed=1 << 23, transcendentals=0),
    )(act.reshape(cube + (8, 512)), down, others)


def slot(h):
    return (h % 2) * 16 + h // 2


def front_kernel(lengths, qn, qr, ka_hbm, ct_hbm, new, va_hbm, w0, w1, w2, w3, out, o0, o1, o2, o3, fresh, ka, ct, va, ropef, ropeb, wide,
                 qs, qg, rg, ats, atg, loads, q_s, q_r, r_s, r_r, a_s, a_r, x_s, x_r):
    x, y, z, c = place()
    e = (x * 4 + z) * 2 + c
    others = [(k - 1, (y + k) % 4) for k in range(1, 4)]
    fetch = [pltpu.make_async_copy(a, b, loads.at[n])
             for n, (a, b) in enumerate(((ka_hbm, ka), (ct_hbm, ct), (va_hbm, va)))]
    for copy in fetch:
        copy.start()
    barrier = pltpu.get_barrier_semaphore()
    for k, t in others:
        pl.semaphore_signal(barrier, inc=1, device_id=(e, t), device_id_type=MESH)
    sib = partner(x, y, z, c, SIBLING)
    pl.semaphore_signal(barrier, inc=1, device_id=sib, device_id_type=MESH)
    pl.semaphore_wait(barrier, 4)
    trade = [pltpu.make_async_remote_copy(
        src_ref=a, dst_ref=b, send_sem=x_s.at[n], recv_sem=x_r.at[n], device_id=sib, device_id_type=MESH)
        for n, (a, b) in enumerate(((w0, o0), (w1, o1), (w2, o2), (w3, o3)))]

    def rope_copy(k, t):
        return pltpu.make_async_remote_copy(
            src_ref=ropeb.at[t], dst_ref=rg.at[y], send_sem=r_s.at[k], recv_sem=r_r.at[k],
            device_id=(e, t), device_id_type=MESH)

    def query_copy(i, k, t):
        return pltpu.make_async_remote_copy(
            src_ref=qs.at[i, t], dst_ref=qg.at[i, y], send_sem=q_s.at[i, k], recv_sem=q_r.at[i, k],
            device_id=(e, t), device_id_type=MESH)

    def back_copy(i, k, t):
        return pltpu.make_async_remote_copy(
            src_ref=ats.at[i, t], dst_ref=atg.at[i, y], send_sem=a_s.at[i, k], recv_sem=a_r.at[i, k],
            device_id=(e, t), device_id_type=MESH)

    fresh[...] = new[...].astype(F32)
    for j in range(16):
        ropef[:, j, :] = qr[:, j * 128:(j + 1) * 128].astype(F32)
    ropeb[...] = ropef[...].astype(BF).reshape(4, 8, 16, 128)
    for k, t in others:
        rope_copy(k, t).start()
    rg[y] = ropeb[y]
    fetch[0].wait()
    for h in range(32):
        wide[:, slot(h), :] = jnp.dot(qn[:, h * 128:(h + 1) * 128], ka[h], preferred_element_type=F32)

    def push(i, carry):
        for k, t in others:
            qs[i, t] = wide[t * 8 + i].astype(BF)
            query_copy(i, k, t).start()
        qg[i, y] = wide[y * 8 + i].astype(BF)
        return carry

    lax.fori_loop(0, 8, push, 0)
    for copy in trade:
        copy.start()
    fetch[1].wait()
    for k, t in others:
        rope_copy(k, t).wait_recv()

    def attend(i, carry):
        for k, t in others:
            query_copy(i, k, t).wait_recv()
        q = qg[i].reshape(128, 512)
        ropes = [rg[t, i] for t in range(4)]
        ropes = jnp.concatenate([half for v in ropes for half in (v[:, :64], v[:, 64:])], axis=0)
        s = jnp.dot(q, ct[i, :512, :], preferred_element_type=F32)
        s = s + jnp.dot(ropes, ct[i, 512:, :], preferred_element_type=F32)
        scale = 1.0 / math.sqrt(192)
        inside = lax.broadcasted_iota(jnp.int32, (128, 512), 1) < lengths[i]
        s = jnp.where(inside, s * scale, -1e30)
        latest = fresh[pl.ds(i, 1), :]
        own = jnp.sum(q.astype(F32) * latest[:, :512], axis=1, keepdims=True)
        own = (own + jnp.sum(ropes.astype(F32) * latest[:, 512:], axis=1, keepdims=True)) * scale
        top = jnp.maximum(jnp.max(s, axis=1, keepdims=True), own)
        w = jnp.exp(s - top)
        own = jnp.exp(own - top)
        total = jnp.sum(w, axis=1, keepdims=True) + own
        a = lax.dot_general(w.astype(BF), ct[i, :512, :], (((1,), (1,)), ((), ())),
                            preferred_element_type=F32)
        a = (a + own * latest[:, :512]) / total
        ats[i] = a.astype(BF).reshape(4, 32, 512)
        for k, t in others:
            back_copy(i, k, t).start()
        atg[i, y] = ats[i, y]
        return carry

    lax.fori_loop(0, 8, attend, 0)

    def widen(i, carry):
        for k, t in others:
            back_copy(i, k, t).wait_recv()
        for t in range(4):
            wide[t * 8 + i] = atg[i, t].astype(F32)
        return carry

    lax.fori_loop(0, 8, widen, 0)
    fetch[2].wait()
    for h in range(32):
        v = wide[:, slot(h), :].astype(BF)
        out[:, h * 128:(h + 1) * 128] = jnp.dot(v, va[h], preferred_element_type=F32).astype(BF)

    def finish(i, carry):
        for k, t in others:
            query_copy(i, k, t).wait_send()
            back_copy(i, k, t).wait_send()
        return carry

    lax.fori_loop(0, 8, finish, 0)
    for k, t in others:
        rope_copy(k, t).wait_send()
    for copy in trade:
        copy.wait()


def front(lengths, qn, qr, ka, ct, new, va, weights, cid):
    inside = pl.BlockSpec(memory_space=pltpu.VMEM)
    outside = pl.BlockSpec(memory_space=pl.ANY)
    dma = lambda *shape: pltpu.SemaphoreType.DMA(shape)
    return pl.pallas_call(
        front_kernel,
        out_shape=(jax.ShapeDtypeStruct((32, 4096), BF),) + tuple(jax.ShapeDtypeStruct(w.shape, BF) for w in weights),
        in_specs=[pl.BlockSpec(memory_space=pltpu.SMEM), inside, inside, outside, outside, inside, outside]
        + [outside] * 4,
        out_specs=(inside,) + (outside,) * 4,
        scratch_shapes=[
            pltpu.VMEM((8, 576), F32),
            pltpu.VMEM((32, 128, 512), BF), pltpu.VMEM((8, 576, 512), BF), pltpu.VMEM((32, 512, 128), BF),
            pltpu.VMEM((32, 16, 128), F32), pltpu.VMEM((4, 8, 16, 128), BF), pltpu.VMEM((32, 32, 512), F32),
            pltpu.VMEM((8, 4, 32, 512), BF), pltpu.VMEM((8, 4, 32, 512), BF), pltpu.VMEM((4, 8, 16, 128), BF),
            pltpu.VMEM((8, 4, 32, 512), BF), pltpu.VMEM((8, 4, 32, 512), BF),
            dma(3), dma(8, 3), dma(8, 3), dma(3), dma(3), dma(8, 3), dma(8, 3), dma(4), dma(4),
        ],
        compiler_params=pltpu.CompilerParams(
            collective_id=cid, has_side_effects=True, vmem_limit_bytes=56 << 20),
        cost_estimate=pl.CostEstimate(flops=1 << 31, bytes_accessed=1 << 24, transcendentals=1 << 19),
    )(lengths, qn, qr, ka, ct, new, va, *weights)


def per_device(
    query_nope,
    query_rope,
    key_absorb,
    latent_cache,
    new_latent,
    context_lengths,
    value_absorb,
    out_proj,
    residual,
    norm_gain,
    routes,
    gate_weights,
    expert_gate,
    expert_up,
    expert_down,
):
    proj = jnp.swapaxes(out_proj, 0, 1)
    gate, up, down = expert_gate[0], expert_up[0], expert_down[0]
    head_out, proj2, gate2, up2, down2 = front(
        context_lengths, query_nope, query_rope, key_absorb, jnp.swapaxes(latent_cache, 1, 2),
        new_latent, value_absorb, (proj, gate, up, down), 0,
    )
    act, own = middle(
        head_out, proj, proj2, residual, norm_gain.reshape(32, 224), routes, gate_weights, (gate, up, gate2, up2), 1
    )
    routed = moe_out(act, down, down2, 2)
    hidden = own[:8].astype(F32) / norm_gain.astype(F32)[None, :]
    return (hidden + routed).astype(BF)


def solution(mesh):
    placed = (
        P("expert", "tensor"),
        P("expert", "tensor"),
        P("tensor", None, None),
        P(("expert", "tensor"), None, None),
        P(("expert", "tensor"), None),
        P(("expert", "tensor")),
        P("tensor", None, None),
        P("tensor", "expert"),
        P(("expert", "tensor"), None),
        P(),
        P(("expert", "tensor"), None),
        P(("expert", "tensor"), None),
        P("expert", None, "tensor"),
        P("expert", None, "tensor"),
        P("expert", "tensor", None),
    )
    return jax.shard_map(
        per_device,
        mesh=mesh,
        in_specs=placed,
        out_specs=P(("expert", "tensor"), None),
        check_vma=False,
    )
```

```python
import functools, math
import jax, jax.numpy as jnp
from jax import lax
from jax.experimental import pallas as pl
from jax.experimental.pallas import tpu as pltpu
from jax.sharding import PartitionSpec as P

MESH = pl.DeviceIdType.MESH
BF = jnp.bfloat16
F32 = jnp.float32
SIBLING = 6


def place():
    e, y = lax.axis_index("expert"), lax.axis_index("tensor")
    return e // 8, y, (e // 2) % 4, e % 2


def cube_bits(x, y, z):
    out = []
    for v in (y, x, z):
        g = jnp.where(v >= 2, 5 - v, v)
        out += [g // 2, g % 2]
    return out


def partner(x, y, z, c, d):
    if d == SIBLING:
        return ((x * 4 + z) * 2 + 1 - c, y)
    at = [y, x, z]
    v = at[d // 2]
    at[d // 2] = 3 - v if d % 2 == 0 else v + 1 - 2 * (v % 2)
    y, x, z = at
    return ((x * 4 + z) * 2 + c, y)


def meet(dims, x, y, z, c):
    barrier = pltpu.get_barrier_semaphore()
    for d in dims:
        pl.semaphore_signal(barrier, inc=1, device_id=partner(x, y, z, c, d), device_id_type=MESH)
    pl.semaphore_wait(barrier, len(dims))


FREE, OTHER, MINE = "free", "other", "mine"


def index_of(bits, spec):
    return [slice(None) if spec.get(d) == FREE else (1 - bits[d] if spec.get(d) == OTHER else bits[d])
            for d in range(6)]


class Gather:
    def __init__(self, order, cut, send_sem, recv_sem, where, split=True):
        self.order, self.cut, self.where, self.split = order, cut, where, split
        self.sems = send_sem, recv_sem
        self.copies = {}

    def send(self, s, part):
        o = self.order
        spec = {d: FREE for d in o[:max(s - 1, 0) if self.split else s]}
        if part:
            spec[o[s - 1]] = OTHER
        ref = self.cut(spec)
        copy = pltpu.make_async_remote_copy(
            src_ref=ref, dst_ref=ref, send_sem=self.sems[0].at[s, part], recv_sem=self.sems[1].at[s, part],
            device_id=partner(*self.where, o[s]), device_id_type=MESH)
        copy.start()
        self.copies[s, part] = copy

    def last(self, part):
        o = self.order
        spec = {d: FREE for d in o[:-2]}
        spec[o[-1]] = OTHER
        if part:
            spec[o[-2]] = OTHER
        return spec

    def turn(self, s):
        if s == 0:
            self.send(0, 0)
            if self.split:
                self.send(1, 0)
            return
        for part in (0, 1) if self.split and s > 1 else (0,):
            self.copies[s - 1, part].wait_recv()
        if s < len(self.order):
            if self.split:
                self.send(s, 1)
                if s + 1 < len(self.order):
                    self.send(s + 1, 0)
            else:
                self.send(s, 0)

    def finish(self, part):
        self.copies[len(self.order) - 1, part].wait_recv()

    def wait_sends(self):
        for copy in self.copies.values():
            copy.wait_send()


ROW_AT = (0, 80, 160, 240, 320, 384)
ROW_N = (80, 80, 80, 80, 64, 64)


def slot(h):
    return (h % 2) * 16 + h // 2


def main_kernel(lengths, qn, qr, ka_hbm, ct_hbm, new, va_hbm, proj_hbm, res, gains, routes, weights, gate_hbm, up_hbm,
                down_hbm, act, own, others,
                fresh, ka, ct, va, ropef, ropeb, wide, qs, qg, rg, ats, atg, proj, wts, heads, product, part, summed,
                gainf, turn, turnf, got, buf, sqb, acc, factors,
                loads, q_s, q_r, r_s, r_r, a_s, a_r, x_s, x_r, h_s, h_r, y_s, y_r, t_s, t_r, st_s, st_r):
    x, y, z, c = where = place()
    bits = cube_bits(x, y, z)
    yh, yl, xh, xl, zh, zl = bits
    chip = (x * 4 + z) * 2
    e = chip + c
    others_y = [(k - 1, (y + k) % 4) for k in range(1, 4)]
    sib = partner(x, y, z, c, SIBLING)
    fetch = [pltpu.make_async_copy(a, b, loads.at[n]) for n, (a, b) in enumerate((
        (ka_hbm, ka), (ct_hbm, ct), (va_hbm, va), (proj_hbm, proj.at[c]), (gate_hbm, wts.at[0, 0]),
        (up_hbm, wts.at[0, 1])))]
    for copy in fetch:
        copy.start()
    barrier = pltpu.get_barrier_semaphore()
    for d in range(7):
        pl.semaphore_signal(barrier, inc=1, device_id=partner(x, y, z, c, d), device_id_type=MESH)
    pl.semaphore_signal(barrier, inc=1, device_id=(e, (y + 2) % 4), device_id_type=MESH)
    fresh[...] = new[...].astype(F32)
    for j in range(16):
        ropef[:, j, :] = qr[:, j * 128:(j + 1) * 128].astype(F32)
    ropeb[...] = ropef[...].astype(BF).reshape(4, 8, 16, 128)
    pl.semaphore_wait(barrier, 8)
    trade = [pltpu.make_async_remote_copy(
        src_ref=a, dst_ref=b, send_sem=x_s.at[n], recv_sem=x_r.at[n], device_id=sib, device_id_type=MESH)
        for n, (a, b) in enumerate((
            (proj_hbm, proj.at[c]), (gate_hbm, wts.at[1, 0]), (up_hbm, wts.at[1, 1]), (down_hbm, others)))]

    def rope_copy(k, t):
        return pltpu.make_async_remote_copy(
            src_ref=ropeb.at[t], dst_ref=rg.at[y], send_sem=r_s.at[k], recv_sem=r_r.at[k],
            device_id=(e, t), device_id_type=MESH)

    def query_copy(i, k, t):
        return pltpu.make_async_remote_copy(
            src_ref=qs.at[i, t], dst_ref=qg.at[i, y], send_sem=q_s.at[i, k], recv_sem=q_r.at[i, k],
            device_id=(e, t), device_id_type=MESH)

    def back_copy(i, k, t):
        return pltpu.make_async_remote_copy(
            src_ref=ats.at[i, t], dst_ref=atg.at[i, y], send_sem=a_s.at[i, k], recv_sem=a_r.at[i, k],
            device_id=(e, t), device_id_type=MESH)

    fresh[...] = new[...].astype(F32)
    for k, t in others_y:
        rope_copy(k, t).start()
    rg[y] = ropeb[y]
    fetch[0].wait()
    for h in range(32):
        wide[:, slot(h), :] = jnp.dot(qn[:, h * 128:(h + 1) * 128], ka[h], preferred_element_type=F32)

    def push(i, carry):
        for k, t in others_y:
            qs[i, t] = wide[t * 8 + i].astype(BF)
            query_copy(i, k, t).start()
        qg[i, y] = wide[y * 8 + i].astype(BF)
        return carry

    lax.fori_loop(0, 4, push, 0)
    for copy in trade:
        copy.start()

    turn[...] = jnp.zeros_like(turn)
    part[...] = jnp.zeros_like(part)
    for k in range(16):
        sx, sz = k // 4 ^ k // 8, k % 4 ^ k % 4 // 2
        v = [res[:, n * 224:(n + 1) * 224].astype(F32) for n in (2 * k, 2 * k + 1)]
        turn[sx // 2, sx % 2, sz // 2, sz % 2, :, :224] = jnp.concatenate(v, axis=0).astype(BF)
    for k in range(32):
        gainf[k:k + 1, :] = gains[:, k * 224:(k + 1) * 224].astype(F32)
    lane = lax.broadcasted_iota(jnp.int32, (8, 128), 1)
    table = jnp.zeros((8, 128), F32)
    for k in range(8):
        table = table + jnp.where(lane == routes[:, k:k + 1], weights[:, k:k + 1], 0.0)
    acc[...] = jnp.zeros_like(acc)
    fetch[1].wait()
    for k, t in others_y:
        rope_copy(k, t).wait_recv()

    def attend(i, carry):
        for k, t in others_y:
            query_copy(i, k, t).wait_recv()
        q = qg[i].reshape(128, 512)
        ropes = [rg[t, i] for t in range(4)]
        ropes = jnp.concatenate([half for v in ropes for half in (v[:, :64], v[:, 64:])], axis=0)
        s = jnp.dot(q, ct[i, :512, :], preferred_element_type=F32)
        s = s + jnp.dot(ropes, ct[i, 512:, :], preferred_element_type=F32)
        scale = 1.0 / math.sqrt(192)
        inside = lax.broadcasted_iota(jnp.int32, (128, 512), 1) < lengths[i]
        s = jnp.where(inside, s * scale, -1e30)
        latest = fresh[pl.ds(i, 1), :]
        own = jnp.sum(q.astype(F32) * latest[:, :512], axis=1, keepdims=True)
        own = (own + jnp.sum(ropes.astype(F32) * latest[:, 512:], axis=1, keepdims=True)) * scale
        top = jnp.maximum(jnp.max(s, axis=1, keepdims=True), own)
        w = jnp.exp(s - top)
        own = jnp.exp(own - top)
        total = jnp.sum(w, axis=1, keepdims=True) + own
        a = lax.dot_general(w.astype(BF), ct[i, :512, :], (((1,), (1,)), ((), ())),
                            preferred_element_type=F32)
        a = (a + own * latest[:, :512]) / total
        ats[i] = a.astype(BF).reshape(4, 32, 512)
        for k, t in others_y:
            back_copy(i, k, t).start()
        atg[i, y] = ats[i, y]
        return carry

    lax.fori_loop(0, 4, attend, 0)
    lax.fori_loop(4, 8, push, 0)

    def head_cut(n, p):
        def cut(spec):
            g = index_of(bits, spec)
            return heads.at[n, g[2], g[3], g[4], g[5], :, pl.ds(p * 1024, 1024)]
        return cut

    first = [[Gather([2 + (p + i) % 4 for i in range(4)], head_cut(n, p), h_s.at[n, p], h_r.at[n, p], where)
              for p in range(4)] for n in range(2)]

    def head_out(n):
        def widen(i, carry):
            for k, t in others_y:
                back_copy(n * 4 + i, k, t).wait_recv()
            for t in range(4):
                wide[n * 16 + t * 4 + i] = atg[n * 4 + i, t].astype(F32)
            return carry

        lax.fori_loop(0, 4, widen, 0)
        for h in range(32):
            v = wide[n * 16:n * 16 + 16, slot(h), :].astype(BF)
            o = jnp.dot(v, va[h], preferred_element_type=F32)
            heads[n, xh, xl, zh, zl, :, h * 128:(h + 1) * 128] = o.astype(BF)

    def residual_turn(k):
        d = 2 + k
        at = tuple(1 - bits[d] if m == d else slice(None) for m in (2, 3, 4, 5))
        copy = pltpu.make_async_remote_copy(
            src_ref=turn.at[at], dst_ref=got.at[k], send_sem=t_s.at[k], recv_sem=t_r.at[k],
            device_id=partner(x, y, z, c, d), device_id_type=MESH)
        copy.start()
        return copy, at

    def project(n):
        v = heads[n].reshape(256, 4096)
        for m in range(2):
            o = lax.dot_general(v, proj[m], (((1,), (1,)), ((), ())), preferred_element_type=F32)
            product[...] = o.reshape(16, 16, 224)
            for t in range(4):
                rows = [product[:, t * 4 + i, :] for i in range(4)]
                part[n, t, m, :, :224] = jnp.concatenate(rows, axis=0).astype(BF)
        copies = []
        for k, t in others_y:
            copy = pltpu.make_async_remote_copy(
                src_ref=part.at[n, t], dst_ref=summed.at[n, k], send_sem=y_s.at[n, k], recv_sem=y_r.at[n, k],
                device_id=(e, t), device_id_type=MESH)
            copy.start()
            copies.append(copy)
        return copies

    fetch[2].wait()
    head_out(0)
    turning = None
    for s in range(4):
        for g in first[0]:
            g.turn(s)
        if turning is not None:
            turning[0].wait()
            turn[turning[1]] = got[s - 1]
        turning = residual_turn(s)
        attend(4 + s, 0)
    head_out(1)
    for s in range(2):
        for g in first[1]:
            g.turn(s)
    for half in range(2):
        for g in first[0]:
            g.finish(half)
    for g in first[1]:
        g.turn(2)
    fetch[3].wait()
    trade[0].wait_recv()
    copies = [project(0)]
    for g in first[1]:
        g.turn(3)
    turning[0].wait()
    turn[turning[1]] = got[3]
    turnf[...] = turn[...].astype(F32).reshape(16, 16, 256)
    for half in range(2):
        for g in first[1]:
            g.finish(half)
    copies.append(project(1))
    sums = []
    for n in range(2):
        total = part[n, y].astype(F32)
        for k, copy in enumerate(copies[n]):
            copy.wait_recv()
            total = total + summed[n, k].astype(F32)
        sums.append(total[:, :, :224].astype(BF).astype(F32))
    squares, hid = 0.0, []
    for m in range(2):
        hidden = jnp.concatenate([sums[0][m], sums[1][m]], axis=0)
        hidden = hidden + jnp.concatenate([turnf[:, m * 8 + i, :224] for i in range(8)], axis=0)
        squares = squares + jnp.sum(hidden * hidden, axis=1, keepdims=True)
        hid.append((hidden * gainf[pl.ds(chip + m, 1), :]).T)
    lane3 = lax.broadcasted_iota(jnp.int32, (8, 16, 128), 2)
    from3 = lax.broadcasted_iota(jnp.int32, (8, 16, 128), 1)
    spread = jnp.sum(jnp.where(lane3 == from3 + 32, squares.reshape(8, 16, 1), 0.0), axis=1)
    sqb[yh, yl, xh, xl, zh, zl] = table + spread
    buf[xh, xl, yh, yl, zh, zl] = jnp.concatenate(hid, axis=0).astype(BF)

    def cut_of(p):
        def cut(spec):
            g = index_of(bits, spec)
            if p == 6:
                return sqb.at[g[0], g[1], g[2], g[3], g[4], g[5]]
            return buf.at[g[2], g[3], g[0], g[1], g[4], g[5], pl.ds(ROW_AT[p], ROW_N[p]), :]
        return cut

    def order_of(p):
        return [((4 if p == 6 else p) + k) % 6 for k in range(6)]

    second = [Gather(order_of(p), cut_of(p), st_s.at[p], st_r.at[p], where, p < 6) for p in range(7)]

    def work(p, spec):
        rows = pl.ds(ROW_AT[p], ROW_N[p])
        opts = [(0, 1) if spec.get(d) == FREE else ((1 - bits[d],) if spec.get(d) == OTHER else (bits[d],))
                for d in range(6)]
        inner = [(i, j, k, l) for i in opts[2] for j in opts[3] for k in opts[4] for l in opts[5]]
        outer = [(a, b) for a in opts[0] for b in opts[1]]
        lhs = []
        for a, b in outer:
            slab = [buf[i, j, a, b, k, l, rows, :] for i, j, k, l in inner]
            lhs.append(jnp.concatenate(slab, axis=0).T)
        lhs = jnp.concatenate(lhs, axis=0)
        for n in range(2):
            for m in range(2):
                v = [wts[n, m, 2 * i + (i + j - 2 * i * j), 2 * k + (k + l - 2 * k * l), rows, :]
                     for i, j, k, l in inner]
                o = jnp.dot(lhs, jnp.concatenate(v, axis=0), preferred_element_type=F32)
                for q, (a, b) in enumerate(outer):
                    acc[n, m, a, b] += o[q * 128:(q + 1) * 128]

    for s in range(6):
        for g in second:
            g.turn(s)
    for copy in fetch[4:]:
        copy.wait()
    for copy in trade[1:3]:
        copy.wait_recv()
    for p in range(6):
        work(p, {d: FREE for d in order_of(p)[:5]})
    second[6].turn(6)
    lane = lax.broadcasted_iota(jnp.int32, (128, 128), 1)
    block = lax.broadcasted_iota(jnp.int32, (128, 128), 0) % 16
    for t in range(4):
        info = jnp.concatenate([sqb[t // 2, t % 2, :, :, :, :, i, :].reshape(16, 128) for i in range(8)], axis=0)
        total = jnp.sum(info.reshape(8, 16, 128), axis=1, keepdims=True)
        total = jnp.broadcast_to(total, (8, 16, 128)).reshape(128, 128)
        total = jnp.sum(jnp.where(lane == block + 32, total, 0.0), axis=1, keepdims=True)
        scale = lax.rsqrt(total / 7168.0 + 1e-6)
        for n in range(2):
            expert = chip + (c if n == 0 else 1 - c)
            wt = jnp.sum(jnp.where(lane == expert, info, 0.0), axis=1, keepdims=True)
            factors[t, n] = jnp.where(lane == 0, scale, wt)
    for half in range(2):
        for p in range(6):
            second[p].finish(half)
            work(p, second[p].last(half))
    for t in range(4):
        for n in range(2):
            scale, wt = factors[t, n, :, 0:1], factors[t, n, :, 1:2]
            g = acc[n, 0, t // 2, t % 2] * scale
            u = acc[n, 1, t // 2, t % 2] * scale
            a = g * u / (1.0 + jnp.exp(-g)) * wt
            for i in range(8):
                act[t * 16:(t + 1) * 16, i, n * 256:(n + 1) * 256] = a[i * 16:(i + 1) * 16]
    spot = (xh * 2 + xl) * 4 + zh * 2 + zl
    row = lax.broadcasted_iota(jnp.int32, (16, 128), 0)
    pick = (lax.broadcasted_iota(jnp.int32, (16, 128), 1) == row * 16 + spot) & (row < 8)
    pick = jnp.where(pick, 1.0, 0.0).astype(BF)
    for j in range(4):
        v = jnp.concatenate([buf[j // 2, j % 2, yh, yl, k // 2, k % 2] for k in (0, 1, 3, 2)], axis=0)
        v = lax.dot_general(pick, v, (((1,), (1,)), ((), ())), preferred_element_type=F32)
        ax = j if j < 2 else 5 - j
        own[:, ax * 1792:(ax + 1) * 1792] = v.astype(BF)

    def finish(i, carry):
        for k, t in others_y:
            query_copy(i, k, t).wait_send()
            back_copy(i, k, t).wait_send()
        return carry

    lax.fori_loop(0, 8, finish, 0)
    for k, t in others_y:
        rope_copy(k, t).wait_send()
    for copy in trade:
        copy.wait_send()
    trade[3].wait_recv()
    for g in first[0] + first[1] + second:
        g.wait_sends()
    for copy in copies[0] + copies[1]:
        copy.wait_send()


def main(lengths, qn, qr, ka, ct, new, va, proj, res, gains, routes, weights, gate, up, down, cid):
    vm = lambda shape, kind=BF: pltpu.VMEM(shape, kind)
    dma = lambda *shape: pltpu.SemaphoreType.DMA(shape)
    two = lambda n: (2,) * n
    inside = pl.BlockSpec(memory_space=pltpu.VMEM)
    outside = pl.BlockSpec(memory_space=pl.ANY)
    return pl.pallas_call(
        main_kernel,
        out_shape=(jax.ShapeDtypeStruct((64, 8, 512), F32), jax.ShapeDtypeStruct((16, 7168), BF),
                   jax.ShapeDtypeStruct(down.shape, BF)),
        in_specs=[pl.BlockSpec(memory_space=pltpu.SMEM), inside, inside, outside, outside, inside, outside, outside]
        + [inside] * 4 + [outside] * 3,
        out_specs=(inside, inside, outside),
        scratch_shapes=[
            vm((8, 576), F32), vm((32, 128, 512)), vm((8, 576, 512)), vm((32, 512, 128)),
            vm((32, 16, 128), F32), vm((4, 8, 16, 128)), vm((32, 32, 512), F32),
            vm((8, 4, 32, 512)), vm((8, 4, 32, 512)), vm((4, 8, 16, 128)),
            vm((8, 4, 32, 512)), vm((8, 4, 32, 512)),
            vm((2, 224, 4096)), vm((2, 2, 4, 4, 448, 256)),
            vm((2,) + two(4) + (16, 4096)), vm((16, 16, 224), F32),
            vm((2, 4, 2, 64, 256)), vm((2, 3, 2, 64, 256)),
            vm((32, 224), F32), vm(two(4) + (16, 256)), vm((16, 16, 256), F32), vm((4,) + two(3) + (16, 256)),
            vm(two(6) + (448, 128)), vm(two(6) + (8, 128), F32), vm((2, 2, 2, 2, 128, 256), F32), vm((4, 2, 128, 128), F32),
            dma(6), dma(8, 3), dma(8, 3), dma(3), dma(3), dma(8, 3), dma(8, 3), dma(4), dma(4),
            dma(2, 4, 4, 2), dma(2, 4, 4, 2), dma(2, 3), dma(2, 3), dma(4), dma(4), dma(7, 6, 2), dma(7, 6, 2),
        ],
        compiler_params=pltpu.CompilerParams(
            collective_id=cid, has_side_effects=True, vmem_limit_bytes=62 << 20),
        cost_estimate=pl.CostEstimate(
            flops=1 << 34, bytes_accessed=1 << 25, transcendentals=1 << 20),
    )(lengths, qn, qr, ka, ct, new, va, proj, res, gains, routes, weights,
      gate.reshape(4, 4, 448, 256), up.reshape(4, 4, 448, 256), down)


OUT_W = (640, 640, 640, 640, 512, 512)
OUT_AT = (0, 640, 1280, 1920, 2560, 3072)


def moe_out_kernel(act, down_hbm, others_hbm, out, down, ps, r0, r1, r2, r3, r4, r5, loads, st_s, st_r):
    x, y, z, c = place()
    bits = cube_bits(x, y, z)
    rs = (r0, r1, r2, r3, r4, r5)
    fetch = []
    for p in range(6):
        for n, at in enumerate((OUT_AT[p], 3584 + OUT_AT[p])):
            for m, ref in enumerate((down_hbm, others_hbm)):
                copy = pltpu.make_async_copy(
                    ref.at[:, pl.ds(at, OUT_W[p])], down.at[pl.ds(m * 256, 256), pl.ds(at, OUT_W[p])],
                    loads.at[p, n * 2 + m])
                copy.start()
                fetch.append(copy)
    meet(range(6), x, y, z, c)

    def cut(ref, p, spec):
        idx = tuple(bits[d] if spec[d] == MINE else (1 - bits[d] if spec[d] == OTHER else slice(None))
                    for d in range(6) if d in spec)
        return ref.at[idx + (slice(None), pl.ds(OUT_AT[p], OUT_W[p]))]

    def spec_of(p, s, which):
        spec = {d: FREE for d in range(6)}
        for k in range(s):
            spec[(p + k) % 6] = MINE
        spec[(p + s) % 6] = OTHER
        if s < 5:
            spec[(p + s + 1) % 6] = OTHER if which == 0 else MINE
        return spec

    def product(p, spec):
        rows = act[tuple(bits[d] if spec[d] == MINE else (1 - bits[d] if spec[d] == OTHER else slice(None))
                         for d in range(6))]
        free = sum(spec[d] == FREE for d in range(6))
        rows = rows.reshape(8 << free, 512).astype(BF)
        halves = []
        for at in (OUT_AT[p], 3584 + OUT_AT[p]):
            o = jnp.dot(rows, down[:, at:at + OUT_W[p]], preferred_element_type=F32)
            halves.append(o.reshape(1 << free, 8, OUT_W[p]))
        got = jnp.concatenate(halves, axis=1).astype(BF)
        cut(ps, p, spec)[...] = got.reshape((2,) * free + (16, OUT_W[p]))

    sends = {}

    def landing(p, s, which):
        spec = spec_of(p, s, which)
        return cut(rs[s], p, {d: spec[d] for d in range(6) if d not in [(p + k) % 6 for k in range(s + 1)]})

    def send(p, s, which):
        copy = pltpu.make_async_remote_copy(
            src_ref=cut(ps, p, spec_of(p, s, which)), dst_ref=landing(p, s, which),
            send_sem=st_s.at[s, p, which], recv_sem=st_r.at[s, p, which],
            device_id=partner(x, y, z, c, (p + s) % 6), device_id_type=MESH)
        copy.start()
        sends[p, s, which] = copy

    def take(p, s, which):
        sends[p, s, which].wait_recv()
        spec = dict(spec_of(p, s, which))
        spec[(p + s) % 6] = MINE
        here, other = cut(ps, p, spec), landing(p, s, which)
        here[...] = (here[...].astype(F32) + other[...].astype(F32)).astype(BF)

    for which in (0, 1):
        for p in range(6):
            if which == 0:
                for copy in fetch[p * 4:p * 4 + 4]:
                    copy.wait()
            product(p, spec_of(p, 0, which))
            send(p, 0, which)
    for p in range(6):
        product(p, {d: MINE if d == p else FREE for d in range(6)})
    for s in range(5):
        for p in range(6):
            take(p, s, 0)
            send(p, s + 1, 0)
            if s < 4:
                send(p, s + 1, 1)
        for p in range(6):
            take(p, s, 1)
    for p in range(6):
        take(p, 5, 0)
    mine = ps[tuple(bits)].astype(F32)
    out[:, :3584] = mine[:8]
    out[:, 3584:] = mine[8:]
    for copy in sends.values():
        copy.wait_send()


def moe_out(act, down, others, cid):
    cube = (2,) * 6
    dma = lambda *shape: pltpu.SemaphoreType.DMA(shape)
    inside = pl.BlockSpec(memory_space=pltpu.VMEM)
    outside = pl.BlockSpec(memory_space=pl.ANY)
    return pl.pallas_call(
        moe_out_kernel,
        out_shape=jax.ShapeDtypeStruct((8, 7168), F32),
        in_specs=[inside, outside, outside],
        out_specs=inside,
        scratch_shapes=[
            pltpu.VMEM((512, 7168), BF),
            pltpu.VMEM(cube + (16, 3584), BF),
        ] + [pltpu.VMEM((2,) * (5 - s) + (16, 3584), BF) for s in range(6)] + [
            dma(6, 4), dma(6, 6, 2), dma(6, 6, 2),
        ],
        compiler_params=pltpu.CompilerParams(
            collective_id=cid, has_side_effects=True, vmem_limit_bytes=56 << 20),
        cost_estimate=pl.CostEstimate(flops=2 * 1024 * 256 * 7168, bytes_accessed=1 << 23, transcendentals=0),
    )(act.reshape(cube + (8, 512)), down, others)


def per_device(
    query_nope,
    query_rope,
    key_absorb,
    latent_cache,
    new_latent,
    context_lengths,
    value_absorb,
    out_proj,
    residual,
    norm_gain,
    routes,
    gate_weights,
    expert_gate,
    expert_up,
    expert_down,
):
    act, own, others = main(
        context_lengths, query_nope, query_rope, key_absorb, jnp.swapaxes(latent_cache, 1, 2), new_latent,
        value_absorb, jnp.swapaxes(out_proj, 0, 1), residual, norm_gain[None, :], routes, gate_weights,
        expert_gate[0], expert_up[0], expert_down[0], 1,
    )
    routed = moe_out(act, expert_down[0], others, 2)
    hidden = own[:8].astype(F32) / norm_gain.astype(F32)[None, :]
    return (hidden + routed).astype(BF)


def solution(mesh):
    placed = (
        P("expert", "tensor"),
        P("expert", "tensor"),
        P("tensor", None, None),
        P(("expert", "tensor"), None, None),
        P(("expert", "tensor"), None),
        P(("expert", "tensor")),
        P("tensor", None, None),
        P("tensor", "expert"),
        P(("expert", "tensor"), None),
        P(),
        P(("expert", "tensor"), None),
        P(("expert", "tensor"), None),
        P("expert", None, "tensor"),
        P("expert", None, "tensor"),
        P("expert", "tensor", None),
    )
    return jax.shard_map(
        per_device,
        mesh=mesh,
        in_specs=placed,
        out_specs=P(("expert", "tensor"), None),
        check_vma=False,
    )
```

```python
import functools, math
import jax, jax.numpy as jnp
from jax import lax
from jax.experimental import pallas as pl
from jax.experimental.pallas import tpu as pltpu
from jax.sharding import PartitionSpec as P

MESH = pl.DeviceIdType.MESH
BF = jnp.bfloat16
F32 = jnp.float32
SIBLING = 6


def place():
    e, y = lax.axis_index("expert"), lax.axis_index("tensor")
    return e // 8, y, (e // 2) % 4, e % 2


def cube_bits(x, y, z):
    out = []
    for v in (y, x, z):
        g = jnp.where(v >= 2, 5 - v, v)
        out += [g // 2, g % 2]
    return out


def partner(x, y, z, c, d):
    if d == SIBLING:
        return ((x * 4 + z) * 2 + 1 - c, y)
    at = [y, x, z]
    v = at[d // 2]
    at[d // 2] = 3 - v if d % 2 == 0 else v + 1 - 2 * (v % 2)
    y, x, z = at
    return ((x * 4 + z) * 2 + c, y)


def meet(dims, x, y, z, c):
    barrier = pltpu.get_barrier_semaphore()
    for d in dims:
        pl.semaphore_signal(barrier, inc=1, device_id=partner(x, y, z, c, d), device_id_type=MESH)
    pl.semaphore_wait(barrier, len(dims))


FREE, OTHER, MINE = "free", "other", "mine"


def index_of(bits, spec):
    return [slice(None) if spec.get(d) == FREE else (1 - bits[d] if spec.get(d) == OTHER else bits[d])
            for d in range(6)]


class Gather:
    def __init__(self, order, cut, send_sem, recv_sem, where, split=True):
        self.order, self.cut, self.where, self.split = order, cut, where, split
        self.sems = send_sem, recv_sem
        self.copies = {}

    def send(self, s, part):
        o = self.order
        spec = {d: FREE for d in o[:max(s - 1, 0) if self.split else s]}
        if part:
            spec[o[s - 1]] = OTHER
        ref = self.cut(spec)
        copy = pltpu.make_async_remote_copy(
            src_ref=ref, dst_ref=ref, send_sem=self.sems[0].at[s, part], recv_sem=self.sems[1].at[s, part],
            device_id=partner(*self.where, o[s]), device_id_type=MESH)
        copy.start()
        self.copies[s, part] = copy

    def last(self, part):
        o = self.order
        spec = {d: FREE for d in o[:-2]}
        spec[o[-1]] = OTHER
        if part:
            spec[o[-2]] = OTHER
        return spec

    def turn(self, s):
        if s == 0:
            self.send(0, 0)
            if self.split:
                self.send(1, 0)
            return
        for part in (0, 1) if self.split and s > 1 else (0,):
            self.copies[s - 1, part].wait_recv()
        if s < len(self.order):
            if self.split:
                self.send(s, 1)
                if s + 1 < len(self.order):
                    self.send(s + 1, 0)
            else:
                self.send(s, 0)

    def finish(self, part):
        self.copies[len(self.order) - 1, part].wait_recv()

    def wait_sends(self):
        for copy in self.copies.values():
            copy.wait_send()


ROW_AT = (0, 80, 160, 240, 320, 384)
ROW_N = (80, 80, 80, 80, 64, 64)


def slot(h):
    return (h % 2) * 16 + h // 2


def main_kernel(lengths, qn, qr, ka_hbm, ct_hbm, new, va_hbm, proj_hbm, res, gains, routes, weights, gate_hbm, up_hbm,
                down_hbm, act, own, others,
                fresh, ka, ct, va, ropef, ropeb, wide, qs, qg, rg, ats, atg, proj, wts, heads, product, part, summed,
                gainf, turn, turnf, got, buf, sqb, acc, factors,
                loads, q_s, q_r, r_s, r_r, a_s, a_r, x_s, x_r, h_s, h_r, y_s, y_r, t_s, t_r, st_s, st_r):
    x, y, z, c = where = place()
    bits = cube_bits(x, y, z)
    yh, yl, xh, xl, zh, zl = bits
    chip = (x * 4 + z) * 2
    e = chip + c
    others_y = [(k - 1, (y + k) % 4) for k in range(1, 4)]
    sib = partner(x, y, z, c, SIBLING)
    fetch = [pltpu.make_async_copy(a, b, loads.at[n]) for n, (a, b) in enumerate((
        (ka_hbm, ka), (ct_hbm, ct), (va_hbm, va), (proj_hbm, proj.at[c]), (gate_hbm, wts.at[0, 0]),
        (up_hbm, wts.at[0, 1])))]
    for copy in fetch:
        copy.start()
    barrier = pltpu.get_barrier_semaphore()
    for d in range(7):
        pl.semaphore_signal(barrier, inc=1, device_id=partner(x, y, z, c, d), device_id_type=MESH)
    pl.semaphore_signal(barrier, inc=1, device_id=(e, (y + 2) % 4), device_id_type=MESH)
    fresh[...] = new[...].astype(F32)
    for j in range(16):
        ropef[:, j, :] = qr[:, j * 128:(j + 1) * 128].astype(F32)
    ropeb[...] = ropef[...].astype(BF).reshape(4, 8, 16, 128)
    pl.semaphore_wait(barrier, 8)
    trade = [pltpu.make_async_remote_copy(
        src_ref=a, dst_ref=b, send_sem=x_s.at[n], recv_sem=x_r.at[n], device_id=sib, device_id_type=MESH)
        for n, (a, b) in enumerate((
            (proj_hbm, proj.at[c]), (gate_hbm, wts.at[1, 0]), (up_hbm, wts.at[1, 1]), (down_hbm, others)))]

    def rope_copy(k, t):
        return pltpu.make_async_remote_copy(
            src_ref=ropeb.at[t], dst_ref=rg.at[y], send_sem=r_s.at[k], recv_sem=r_r.at[k],
            device_id=(e, t), device_id_type=MESH)

    def query_copy(i, k, t):
        return pltpu.make_async_remote_copy(
            src_ref=qs.at[i, t], dst_ref=qg.at[i, y], send_sem=q_s.at[i, k], recv_sem=q_r.at[i, k],
            device_id=(e, t), device_id_type=MESH)

    def back_copy(i, k, t):
        return pltpu.make_async_remote_copy(
            src_ref=ats.at[i, t], dst_ref=atg.at[i, y], send_sem=a_s.at[i, k], recv_sem=a_r.at[i, k],
            device_id=(e, t), device_id_type=MESH)

    fresh[...] = new[...].astype(F32)
    for k, t in others_y:
        rope_copy(k, t).start()
    rg[y] = ropeb[y]
    fetch[0].wait()
    for h in range(32):
        wide[:, slot(h), :] = jnp.dot(qn[:, h * 128:(h + 1) * 128], ka[h], preferred_element_type=F32)

    def push(i, carry):
        for k, t in others_y:
            qs[i, t] = wide[t * 8 + i].astype(BF)
            query_copy(i, k, t).start()
        qg[i, y] = wide[y * 8 + i].astype(BF)
        return carry

    lax.fori_loop(0, 4, push, 0)
    for copy in trade:
        copy.start()

    turn[...] = jnp.zeros_like(turn)
    part[...] = jnp.zeros_like(part)
    for k in range(16):
        sx, sz = k // 4 ^ k // 8, k % 4 ^ k % 4 // 2
        v = [res[:, n * 224:(n + 1) * 224].astype(F32) for n in (2 * k, 2 * k + 1)]
        turn[sx // 2, sx % 2, sz // 2, sz % 2, :, :224] = jnp.concatenate(v, axis=0).astype(BF)
    for k in range(32):
        gainf[k:k + 1, :] = gains[:, k * 224:(k + 1) * 224].astype(F32)
    lane = lax.broadcasted_iota(jnp.int32, (8, 128), 1)
    table = jnp.zeros((8, 128), F32)
    for k in range(8):
        table = table + jnp.where(lane == routes[:, k:k + 1], weights[:, k:k + 1], 0.0)
    acc[...] = jnp.zeros_like(acc)
    fetch[1].wait()
    for k, t in others_y:
        rope_copy(k, t).wait_recv()

    def attend(i, carry):
        for k, t in others_y:
            query_copy(i, k, t).wait_recv()
        q = qg[i].reshape(128, 512)
        ropes = [rg[t, i] for t in range(4)]
        ropes = jnp.concatenate([half for v in ropes for half in (v[:, :64], v[:, 64:])], axis=0)
        s = jnp.dot(q, ct[i, :512, :], preferred_element_type=F32)
        s = s + jnp.dot(ropes, ct[i, 512:, :], preferred_element_type=F32)
        scale = 1.0 / math.sqrt(192)
        inside = lax.broadcasted_iota(jnp.int32, (128, 512), 1) < lengths[i]
        s = jnp.where(inside, s * scale, -1e30)
        latest = fresh[pl.ds(i, 1), :]
        own = jnp.sum(q.astype(F32) * latest[:, :512], axis=1, keepdims=True)
        own = (own + jnp.sum(ropes.astype(F32) * latest[:, 512:], axis=1, keepdims=True)) * scale
        top = jnp.maximum(jnp.max(s, axis=1, keepdims=True), own)
        w = jnp.exp(s - top)
        own = jnp.exp(own - top)
        total = jnp.sum(w, axis=1, keepdims=True) + own
        a = lax.dot_general(w.astype(BF), ct[i, :512, :], (((1,), (1,)), ((), ())),
                            preferred_element_type=F32)
        a = (a + own * latest[:, :512]) / total
        ats[i] = a.astype(BF).reshape(4, 32, 512)
        for k, t in others_y:
            back_copy(i, k, t).start()
        atg[i, y] = ats[i, y]
        return carry

    def residual_turn(k):
        d = 2 + k
        at = tuple(1 - bits[d] if m == d else slice(None) for m in (2, 3, 4, 5))
        copy = pltpu.make_async_remote_copy(
            src_ref=turn.at[at], dst_ref=got.at[k], send_sem=t_s.at[k], recv_sem=t_r.at[k],
            device_id=partner(x, y, z, c, d), device_id_type=MESH)
        copy.start()
        return copy, at

    turning = residual_turn(0)
    lax.fori_loop(0, 4, attend, 0)
    turning[0].wait()
    turn[turning[1]] = got[0]
    turning = residual_turn(1)
    lax.fori_loop(4, 8, push, 0)

    def head_cut(n, p):
        def cut(spec):
            g = index_of(bits, spec)
            return heads.at[n, g[2], g[3], g[4], g[5], :, pl.ds(p * 1024, 1024)]
        return cut

    first = [[Gather([2 + (p + i) % 4 for i in range(4)], head_cut(n, p), h_s.at[n, p], h_r.at[n, p], where)
              for p in range(4)] for n in range(2)]

    def head_out(n):
        def widen(i, carry):
            for k, t in others_y:
                back_copy(n * 4 + i, k, t).wait_recv()
            for t in range(4):
                wide[n * 16 + t * 4 + i] = atg[n * 4 + i, t].astype(F32)
            return carry

        lax.fori_loop(0, 4, widen, 0)
        for h in range(32):
            v = wide[n * 16:n * 16 + 16, slot(h), :].astype(BF)
            o = jnp.dot(v, va[h], preferred_element_type=F32)
            heads[n, xh, xl, zh, zl, :, h * 128:(h + 1) * 128] = o.astype(BF)

    def project(n):
        v = heads[n].reshape(256, 4096)
        for m in range(2):
            o = lax.dot_general(v, proj[m], (((1,), (1,)), ((), ())), preferred_element_type=F32)
            product[...] = o.reshape(16, 16, 224)
            for t in range(4):
                rows = [product[:, t * 4 + i, :] for i in range(4)]
                part[n, t, m, :, :224] = jnp.concatenate(rows, axis=0).astype(BF)
        copies = []
        for k, t in others_y:
            copy = pltpu.make_async_remote_copy(
                src_ref=part.at[n, t], dst_ref=summed.at[n, k], send_sem=y_s.at[n, k], recv_sem=y_r.at[n, k],
                device_id=(e, t), device_id_type=MESH)
            copy.start()
            copies.append(copy)
        return copies

    fetch[2].wait()
    head_out(0)
    for s in range(4):
        for g in first[0]:
            g.turn(s)
        if s < 2:
            turning[0].wait()
            turn[turning[1]] = got[s + 1]
            turning = residual_turn(2 + s)
        attend(4 + s, 0)
    head_out(1)
    for s in range(2):
        for g in first[1]:
            g.turn(s)
    for half in range(2):
        for g in first[0]:
            g.finish(half)
    for g in first[1]:
        g.turn(2)
    fetch[3].wait()
    trade[0].wait_recv()
    copies = [project(0)]
    for g in first[1]:
        g.turn(3)
    turning[0].wait()
    turn[turning[1]] = got[3]
    turnf[...] = turn[...].astype(F32).reshape(16, 16, 256)
    for half in range(2):
        for g in first[1]:
            g.finish(half)
    copies.append(project(1))
    sums = []
    for n in range(2):
        total = part[n, y].astype(F32)
        for k, copy in enumerate(copies[n]):
            copy.wait_recv()
            total = total + summed[n, k].astype(F32)
        sums.append(total[:, :, :224].astype(BF).astype(F32))
    squares, hid = 0.0, []
    for m in range(2):
        hidden = jnp.concatenate([sums[0][m], sums[1][m]], axis=0)
        hidden = hidden + jnp.concatenate([turnf[:, m * 8 + i, :224] for i in range(8)], axis=0)
        squares = squares + jnp.sum(hidden * hidden, axis=1, keepdims=True)
        hid.append((hidden * gainf[pl.ds(chip + m, 1), :]).T)
    lane3 = lax.broadcasted_iota(jnp.int32, (8, 16, 128), 2)
    from3 = lax.broadcasted_iota(jnp.int32, (8, 16, 128), 1)
    spread = jnp.sum(jnp.where(lane3 == from3 + 32, squares.reshape(8, 16, 1), 0.0), axis=1)
    sqb[yh, yl, xh, xl, zh, zl] = table + spread
    buf[xh, xl, yh, yl, zh, zl] = jnp.concatenate(hid, axis=0).astype(BF)

    def cut_of(p):
        def cut(spec):
            g = index_of(bits, spec)
            if p == 6:
                return sqb.at[g[0], g[1], g[2], g[3], g[4], g[5]]
            return buf.at[g[2], g[3], g[0], g[1], g[4], g[5], pl.ds(ROW_AT[p], ROW_N[p]), :]
        return cut

    def order_of(p):
        return [((4 if p == 6 else p) + k) % 6 for k in range(6)]

    second = [Gather(order_of(p), cut_of(p), st_s.at[p], st_r.at[p], where, p < 6) for p in range(7)]

    def work(p, spec):
        rows = pl.ds(ROW_AT[p], ROW_N[p])
        opts = [(0, 1) if spec.get(d) == FREE else ((1 - bits[d],) if spec.get(d) == OTHER else (bits[d],))
                for d in range(6)]
        inner = [(i, j, k, l) for i in opts[2] for j in opts[3] for k in opts[4] for l in opts[5]]
        outer = [(a, b) for a in opts[0] for b in opts[1]]
        lhs = []
        for a, b in outer:
            slab = [buf[i, j, a, b, k, l, rows, :] for i, j, k, l in inner]
            lhs.append(jnp.concatenate(slab, axis=0).T)
        lhs = jnp.concatenate(lhs, axis=0)
        for n in range(2):
            for m in range(2):
                v = [wts[n, m, 2 * i + (i + j - 2 * i * j), 2 * k + (k + l - 2 * k * l), rows, :]
                     for i, j, k, l in inner]
                o = jnp.dot(lhs, jnp.concatenate(v, axis=0), preferred_element_type=F32)
                for q, (a, b) in enumerate(outer):
                    acc[n, m, a, b] += o[q * 128:(q + 1) * 128]

    for s in range(6):
        for g in second:
            g.turn(s)
    for copy in fetch[4:]:
        copy.wait()
    for copy in trade[1:3]:
        copy.wait_recv()
    for p in range(6):
        work(p, {d: FREE for d in order_of(p)[:5]})
    second[6].turn(6)
    lane = lax.broadcasted_iota(jnp.int32, (128, 128), 1)
    block = lax.broadcasted_iota(jnp.int32, (128, 128), 0) % 16
    for t in range(4):
        info = jnp.concatenate([sqb[t // 2, t % 2, :, :, :, :, i, :].reshape(16, 128) for i in range(8)], axis=0)
        total = jnp.sum(info.reshape(8, 16, 128), axis=1, keepdims=True)
        total = jnp.broadcast_to(total, (8, 16, 128)).reshape(128, 128)
        total = jnp.sum(jnp.where(lane == block + 32, total, 0.0), axis=1, keepdims=True)
        scale = lax.rsqrt(total / 7168.0 + 1e-6)
        for n in range(2):
            expert = chip + (c if n == 0 else 1 - c)
            wt = jnp.sum(jnp.where(lane == expert, info, 0.0), axis=1, keepdims=True)
            factors[t, n] = jnp.where(lane == 0, scale, wt)
    for half in range(2):
        for p in range(6):
            second[p].finish(half)
            work(p, second[p].last(half))
    for t in range(4):
        for n in range(2):
            scale, wt = factors[t, n, :, 0:1], factors[t, n, :, 1:2]
            g = acc[n, 0, t // 2, t % 2] * scale
            u = acc[n, 1, t // 2, t % 2] * scale
            a = g * u / (1.0 + jnp.exp(-g)) * wt
            for i in range(8):
                act[t * 16:(t + 1) * 16, i, n * 256:(n + 1) * 256] = a[i * 16:(i + 1) * 16]
    spot = (xh * 2 + xl) * 4 + zh * 2 + zl
    row = lax.broadcasted_iota(jnp.int32, (16, 128), 0)
    pick = (lax.broadcasted_iota(jnp.int32, (16, 128), 1) == row * 16 + spot) & (row < 8)
    pick = jnp.where(pick, 1.0, 0.0).astype(BF)
    for j in range(4):
        v = jnp.concatenate([buf[j // 2, j % 2, yh, yl, k // 2, k % 2] for k in (0, 1, 3, 2)], axis=0)
        v = lax.dot_general(pick, v, (((1,), (1,)), ((), ())), preferred_element_type=F32)
        ax = j if j < 2 else 5 - j
        own[:, ax * 1792:(ax + 1) * 1792] = v.astype(BF)

    def finish(i, carry):
        for k, t in others_y:
            query_copy(i, k, t).wait_send()
            back_copy(i, k, t).wait_send()
        return carry

    lax.fori_loop(0, 8, finish, 0)
    for k, t in others_y:
        rope_copy(k, t).wait_send()
    for copy in trade:
        copy.wait_send()
    trade[3].wait_recv()
    for g in first[0] + first[1] + second:
        g.wait_sends()
    for copy in copies[0] + copies[1]:
        copy.wait_send()


def main(lengths, qn, qr, ka, ct, new, va, proj, res, gains, routes, weights, gate, up, down, cid):
    vm = lambda shape, kind=BF: pltpu.VMEM(shape, kind)
    dma = lambda *shape: pltpu.SemaphoreType.DMA(shape)
    two = lambda n: (2,) * n
    inside = pl.BlockSpec(memory_space=pltpu.VMEM)
    outside = pl.BlockSpec(memory_space=pl.ANY)
    return pl.pallas_call(
        main_kernel,
        out_shape=(jax.ShapeDtypeStruct((64, 8, 512), F32), jax.ShapeDtypeStruct((16, 7168), BF),
                   jax.ShapeDtypeStruct(down.shape, BF)),
        in_specs=[pl.BlockSpec(memory_space=pltpu.SMEM), inside, inside, outside, outside, inside, outside, outside]
        + [inside] * 4 + [outside] * 3,
        out_specs=(inside, inside, outside),
        scratch_shapes=[
            vm((8, 576), F32), vm((32, 128, 512)), vm((8, 576, 512)), vm((32, 512, 128)),
            vm((32, 16, 128), F32), vm((4, 8, 16, 128)), vm((32, 32, 512), F32),
            vm((8, 4, 32, 512)), vm((8, 4, 32, 512)), vm((4, 8, 16, 128)),
            vm((8, 4, 32, 512)), vm((8, 4, 32, 512)),
            vm((2, 224, 4096)), vm((2, 2, 4, 4, 448, 256)),
            vm((2,) + two(4) + (16, 4096)), vm((16, 16, 224), F32),
            vm((2, 4, 2, 64, 256)), vm((2, 3, 2, 64, 256)),
            vm((32, 224), F32), vm(two(4) + (16, 256)), vm((16, 16, 256), F32), vm((4,) + two(3) + (16, 256)),
            vm(two(6) + (448, 128)), vm(two(6) + (8, 128), F32), vm((2, 2, 2, 2, 128, 256), F32), vm((4, 2, 128, 128), F32),
            dma(6), dma(8, 3), dma(8, 3), dma(3), dma(3), dma(8, 3), dma(8, 3), dma(4), dma(4),
            dma(2, 4, 4, 2), dma(2, 4, 4, 2), dma(2, 3), dma(2, 3), dma(4), dma(4), dma(7, 6, 2), dma(7, 6, 2),
        ],
        compiler_params=pltpu.CompilerParams(
            collective_id=cid, has_side_effects=True, vmem_limit_bytes=62 << 20),
        cost_estimate=pl.CostEstimate(
            flops=1 << 34, bytes_accessed=1 << 25, transcendentals=1 << 20),
    )(lengths, qn, qr, ka, ct, new, va, proj, res, gains, routes, weights,
      gate.reshape(4, 4, 448, 256), up.reshape(4, 4, 448, 256), down)


OUT_W = (640, 640, 640, 640, 512, 512)
OUT_AT = (0, 640, 1280, 1920, 2560, 3072)


def moe_out_kernel(act, down_hbm, others_hbm, out, down, ps, r0, r1, r2, r3, r4, r5, loads, st_s, st_r):
    x, y, z, c = place()
    bits = cube_bits(x, y, z)
    rs = (r0, r1, r2, r3, r4, r5)
    fetch = []
    for p in range(6):
        for n, at in enumerate((OUT_AT[p], 3584 + OUT_AT[p])):
            for m, ref in enumerate((down_hbm, others_hbm)):
                copy = pltpu.make_async_copy(
                    ref.at[:, pl.ds(at, OUT_W[p])], down.at[pl.ds(m * 256, 256), pl.ds(at, OUT_W[p])],
                    loads.at[p, n * 2 + m])
                copy.start()
                fetch.append(copy)
    meet(range(6), x, y, z, c)

    def cut(ref, p, spec):
        idx = tuple(bits[d] if spec[d] == MINE else (1 - bits[d] if spec[d] == OTHER else slice(None))
                    for d in range(6) if d in spec)
        return ref.at[idx + (slice(None), pl.ds(OUT_AT[p], OUT_W[p]))]

    def spec_of(p, s, which):
        spec = {d: FREE for d in range(6)}
        for k in range(s):
            spec[(p + k) % 6] = MINE
        spec[(p + s) % 6] = OTHER
        if s < 5:
            spec[(p + s + 1) % 6] = OTHER if which == 0 else MINE
        return spec

    def product(p, spec):
        rows = act[tuple(bits[d] if spec[d] == MINE else (1 - bits[d] if spec[d] == OTHER else slice(None))
                         for d in range(6))]
        free = sum(spec[d] == FREE for d in range(6))
        rows = rows.reshape(8 << free, 512).astype(BF)
        halves = []
        for at in (OUT_AT[p], 3584 + OUT_AT[p]):
            o = jnp.dot(rows, down[:, at:at + OUT_W[p]], preferred_element_type=F32)
            halves.append(o.reshape(1 << free, 8, OUT_W[p]))
        got = jnp.concatenate(halves, axis=1).astype(BF)
        cut(ps, p, spec)[...] = got.reshape((2,) * free + (16, OUT_W[p]))

    sends = {}

    def landing(p, s, which):
        spec = spec_of(p, s, which)
        return cut(rs[s], p, {d: spec[d] for d in range(6) if d not in [(p + k) % 6 for k in range(s + 1)]})

    def send(p, s, which):
        copy = pltpu.make_async_remote_copy(
            src_ref=cut(ps, p, spec_of(p, s, which)), dst_ref=landing(p, s, which),
            send_sem=st_s.at[s, p, which], recv_sem=st_r.at[s, p, which],
            device_id=partner(x, y, z, c, (p + s) % 6), device_id_type=MESH)
        copy.start()
        sends[p, s, which] = copy

    def take(p, s, which):
        sends[p, s, which].wait_recv()
        spec = dict(spec_of(p, s, which))
        spec[(p + s) % 6] = MINE
        here, other = cut(ps, p, spec), landing(p, s, which)
        here[...] = (here[...].astype(F32) + other[...].astype(F32)).astype(BF)

    for which in (0, 1):
        for p in range(6):
            if which == 0:
                for copy in fetch[p * 4:p * 4 + 4]:
                    copy.wait()
            product(p, spec_of(p, 0, which))
            send(p, 0, which)
    for p in range(6):
        product(p, {d: MINE if d == p else FREE for d in range(6)})
    for s in range(5):
        for p in range(6):
            take(p, s, 0)
            send(p, s + 1, 0)
            if s < 4:
                send(p, s + 1, 1)
        for p in range(6):
            take(p, s, 1)
    for p in range(6):
        take(p, 5, 0)
    mine = ps[tuple(bits)].astype(F32)
    out[:, :3584] = mine[:8]
    out[:, 3584:] = mine[8:]
    for copy in sends.values():
        copy.wait_send()


def moe_out(act, down, others, cid):
    cube = (2,) * 6
    dma = lambda *shape: pltpu.SemaphoreType.DMA(shape)
    inside = pl.BlockSpec(memory_space=pltpu.VMEM)
    outside = pl.BlockSpec(memory_space=pl.ANY)
    return pl.pallas_call(
        moe_out_kernel,
        out_shape=jax.ShapeDtypeStruct((8, 7168), F32),
        in_specs=[inside, outside, outside],
        out_specs=inside,
        scratch_shapes=[
            pltpu.VMEM((512, 7168), BF),
            pltpu.VMEM(cube + (16, 3584), BF),
        ] + [pltpu.VMEM((2,) * (5 - s) + (16, 3584), BF) for s in range(6)] + [
            dma(6, 4), dma(6, 6, 2), dma(6, 6, 2),
        ],
        compiler_params=pltpu.CompilerParams(
            collective_id=cid, has_side_effects=True, vmem_limit_bytes=56 << 20),
        cost_estimate=pl.CostEstimate(flops=2 * 1024 * 256 * 7168, bytes_accessed=1 << 23, transcendentals=0),
    )(act.reshape(cube + (8, 512)), down, others)


def per_device(
    query_nope,
    query_rope,
    key_absorb,
    latent_cache,
    new_latent,
    context_lengths,
    value_absorb,
    out_proj,
    residual,
    norm_gain,
    routes,
    gate_weights,
    expert_gate,
    expert_up,
    expert_down,
):
    act, own, others = main(
        context_lengths, query_nope, query_rope, key_absorb, jnp.swapaxes(latent_cache, 1, 2), new_latent,
        value_absorb, jnp.swapaxes(out_proj, 0, 1), residual, norm_gain[None, :], routes, gate_weights,
        expert_gate[0], expert_up[0], expert_down[0], 1,
    )
    routed = moe_out(act, expert_down[0], others, 2)
    hidden = own[:8].astype(F32) / norm_gain.astype(F32)[None, :]
    return (hidden + routed).astype(BF)


def solution(mesh):
    placed = (
        P("expert", "tensor"),
        P("expert", "tensor"),
        P("tensor", None, None),
        P(("expert", "tensor"), None, None),
        P(("expert", "tensor"), None),
        P(("expert", "tensor")),
        P("tensor", None, None),
        P("tensor", "expert"),
        P(("expert", "tensor"), None),
        P(),
        P(("expert", "tensor"), None),
        P(("expert", "tensor"), None),
        P("expert", None, "tensor"),
        P("expert", None, "tensor"),
        P("expert", "tensor", None),
    )
    return jax.shard_map(
        per_device,
        mesh=mesh,
        in_specs=placed,
        out_specs=P(("expert", "tensor"), None),
        check_vma=False,
    )
```
